128 devices in a mesh: prompt: 8 (over y_lo, z), resp: 16 (over y_hi, x, core).
Axes of the slice: x: 4, y: 4 (y_hi: 2, y_lo: 2; y = y_hi * 2 + y_lo), z: 4, core: 2. Of those that a mesh axis runs over, the one named last changes fastest.
Arguments:
- queries: bfloat16 [8, 32, 64, 2048], P('prompt', 'resp'), may hold values from -160 to 160
- response_keys: bfloat16 [8, 32, 64, 256], P('prompt', 'resp'), may hold values from -6 to 6
- response_values: bfloat16 [8, 32, 64, 256], P('prompt', 'resp'), may hold values from -6 to 6
- prefix_keys: bfloat16 [8, 512, 256], P('prompt', 'resp'), may hold values from -6 to 6
- prompt_values: bfloat16 [8, 512, 256], P('prompt', 'resp'), may hold values from -6 to 6
- resid: bfloat16 [8, 32, 64, 2048], P('prompt', 'resp'), may hold values from -6 to 6
- out_proj: bfloat16 [2048, 2048], P('prompt'), may hold values from -0.125 to 0.125
- router: bfloat16 [2048, 128], replicated, may hold values from -0.125 to 0.125
- norm_gain: float32 [2048], replicated, may hold values from 0.1 to 1.9
- w_gate: bfloat16 [128, 2048, 768], P(('prompt', 'resp')), may hold values from -0.125 to 0.125
- w_up: bfloat16 [128, 2048, 768], P(('prompt', 'resp')), may hold values from -0.125 to 0.125
- w_down: bfloat16 [128, 768, 2048], P(('prompt', 'resp')), may hold values from -0.21875 to 0.21875
- expert_ids: int32 [8, 32, 64, 4], P('prompt', 'resp'), may hold values from 0 to 127, all different within a row; in each aligned block of 128 rows (0 to 127, 128 to 255, ..., all dimensions but the last counted through in order) at most 6 rows name the same one
- lengths: int32 [8, 32], P('prompt', 'resp'), may hold values from 16 to 64, as said below
- out_grad: bfloat16 [8, 32, 64, 2048], P('prompt', 'resp'), may hold values from -6 to 6
Outputs:
- layer_out: bfloat16 [8, 32, 64, 2048], P('prompt', 'resp')
- resid_grad: bfloat16 [8, 32, 64, 2048], P('prompt', 'resp')
- query_grad: bfloat16 [8, 32, 64, 2048], P('prompt', 'resp')
- resp_key_grad: bfloat16 [8, 32, 64, 256], P('prompt', 'resp')
- resp_value_grad: bfloat16 [8, 32, 64, 256], P('prompt', 'resp')
- prefix_key_grad: bfloat16 [8, 512, 256], P('prompt', 'resp')
- prefix_value_grad: bfloat16 [8, 512, 256], P('prompt', 'resp')
- router_grad: float32 [2048, 128], replicated
- gain_grad: float32 [2048], replicated
- gate_grad: bfloat16 [128, 2048, 768], P(('prompt', 'resp'))
- up_grad: bfloat16 [128, 2048, 768], P(('prompt', 'resp'))
- down_grad: bfloat16 [128, 768, 2048], P(('prompt', 'resp'))
The draws below stay inside these ranges and needn't reach their ends.
Inputs may be any that keep to these rules, and one draw needn't show every extreme that they name: `expert_ids`: among the rows of one device no expert is named by more than 6 rows, a bound that some block reaches; the experts of a row differ. `lengths`: every prompt has a response of 64 positions.
All inputs are finite; a program needn't handle non-finite values.
Results may differ from the reference program's by a relative error of at most 0.039.
Values may be sent and summed in bfloat16 or wider, within the bound.
No kernel may reach another device: no remote copies, remote signals or barrier semaphores. Data moves between devices by JAX's collectives and lax.ppermute only.
A program may use at most 192 MiB of HBM per device.

```python
import math
import jax
import jax.numpy as jnp
import numpy as np
from jax import lax

D = 2048
QUERY_HEADS = 16
KEY_VALUE_HEADS = 2
HEAD_SIZE = 128
FF = 768
TOPK = 4
PROMPT_LENGTH = 512
RESPONSE_LENGTH = 64
RESP_DEV = 2
PROMPT_COUNT = 8
RESPONSE_COUNT = 32
EXPERTS = 128
CAP = 6
N_RESP = 16


def shared_keys(key):
    return jnp.clip(jax.random.normal(key, (PROMPT_COUNT, PROMPT_LENGTH, KEY_VALUE_HEADS, HEAD_SIZE), jnp.float32), -6.0, 6.0)


def draw_prefix_keys(key, part):
    base_offset = shared_keys(key)
    return base_offset.reshape(PROMPT_COUNT, PROMPT_LENGTH, KEY_VALUE_HEADS * HEAD_SIZE).astype(jnp.bfloat16)


def draw_queries(key, part):
    key = jax.random.fold_in(key, 3)
    fresh = jnp.clip(jax.random.normal(key, (PROMPT_COUNT, RESPONSE_COUNT, RESPONSE_LENGTH, QUERY_HEADS, HEAD_SIZE), jnp.float32), -6.0, 6.0)
    return fresh.reshape(PROMPT_COUNT, RESPONSE_COUNT, RESPONSE_LENGTH, QUERY_HEADS * HEAD_SIZE).astype(jnp.bfloat16)


def draw_lengths(key, part):
    key = jax.random.fold_in(key, 9)
    drawn = jax.random.randint(key, (PROMPT_COUNT, RESPONSE_COUNT), RESPONSE_LENGTH // 4, RESPONSE_LENGTH + 1, jnp.int32)
    longest = jax.random.randint(jax.random.fold_in(key, 1), (PROMPT_COUNT,), 0, RESPONSE_COUNT, jnp.int32)
    return jnp.where(jnp.arange(RESPONSE_COUNT, dtype=jnp.int32)[None, :] == longest[:, None], RESPONSE_LENGTH, drawn).astype(jnp.int32)


def steps_of(stream_key, dims, cuts, least, top_value):
    level, own = 1.0, jax.random.fold_in(stream_key, 6)
    for axis_at, shards_of in cuts:
        heights = jnp.exp(jax.random.uniform(jax.random.fold_in(own, axis_at), (shards_of,), jnp.float32, least / len(cuts), top_value / len(cuts)))
        level = level * jnp.repeat(heights, dims[axis_at] // shards_of).reshape([-1 if axis == axis_at else 1 for axis in range(len(dims))])
    return level


def assign_block(own_key, own, number, rows, count, top, limit, skew):
    sequence = jax.random.permutation(own_key, count)
    crowded, usual = portions_of(count, rows * top, limit, skew, True), portions_of(count, rows * top, limit, skew, False)
    places = jnp.arange(count)

    def named(sizes, turn):
        used = int((sizes > 0).sum())
        fixed = max(1, used // 4)
        moved = fixed + (places - fixed + turn * (used - fixed)) % max(1, count - fixed)
        return jnp.zeros((count,), jnp.int32).at[sequence[jnp.where(places < fixed, places, moved)]].set(jnp.asarray(sizes, jnp.int32))

    sizes = jnp.where(number % 4 == 0, named(crowded, number // 4), named(usual, number - number // 4 - 1))
    mixed = jax.random.permutation(jax.random.fold_in(own, 3), count)
    giver, taker = mixed[0:count // 2 * 2:2], mixed[1:count // 2 * 2:2]
    slack = jnp.minimum(sizes[giver] - 1, limit - sizes[taker]) // 2
    slack = jnp.where((giver == sequence[0]) | (taker == sequence[0]) | (sizes[taker] == 0), 0, jnp.maximum(slack, 0))
    moved = jax.random.randint(jax.random.fold_in(own, 4), (count // 2,), 0, 1 << 20) % (slack + 1)
    sizes = sizes.at[giver].add(-moved).at[taker].add(moved)
    members = jnp.searchsorted(jnp.cumsum(sizes), jnp.arange(rows * top), side="right").astype(jnp.int32)
    table = members.reshape(top, rows).T
    table = table[jax.random.permutation(jax.random.fold_in(own, 1), rows)]
    turn = jax.random.randint(jax.random.fold_in(own, 2), (rows, 1), 0, top)
    return jnp.take_along_axis(table, (jnp.arange(top)[None, :] + turn) % top, axis=1)


def portions_of(amount, total, bound, skew, full):
    weights = [(1 << 20) // math.isqrt(grade ** skew) + 1 for grade in range(1, amount + 1)]
    largest = bound if full else min(bound, max(-(-total // amount), total * weights[0] // sum(weights)))
    least = 1 if total - largest >= amount - 1 else 0
    given, spare = [largest] + [least] * (amount - 1), total - largest - least * (amount - 1)
    while spare > 0:
        candidates = [i for i in range(1, amount) if given[i] < largest] or [i for i in range(1, amount) if given[i] < bound]
        whole, left = sum([weights[i] for i in candidates]), spare
        for i in candidates:
            extra = min(bound - given[i], max(1, left * weights[i] // whole), spare)
            given[i] = given[i] + extra
            spare = spare - extra
    return np.array(given)


def noise(stream_key, extent, width, most, split=(), kind=jnp.bfloat16):
    level = steps_of(stream_key, extent, split, -0.22, 0.18) if split else 1.0
    entries = jax.random.normal(stream_key, extent, jnp.float32) * width * level
    return jnp.minimum(jnp.maximum(entries, -most), most).astype(kind)


def setup_inputs(seed: int = 0) -> dict:
    key_of = jax.random.split(jax.random.key(seed), 16)
    queries = draw_queries(jax.random.fold_in(key_of[15], 71), 0)
    response_keys = noise(key_of[1], (PROMPT_COUNT, RESPONSE_COUNT, RESPONSE_LENGTH, KEY_VALUE_HEADS * HEAD_SIZE), 1.0, 6.0, ((0, 8), (1, 16)))
    response_values = noise(key_of[2], (PROMPT_COUNT, RESPONSE_COUNT, RESPONSE_LENGTH, KEY_VALUE_HEADS * HEAD_SIZE), 1.0, 6.0, ((0, 8), (1, 16)))
    prefix_keys = draw_prefix_keys(jax.random.fold_in(key_of[15], 71), 0)
    prompt_values = noise(key_of[4], (PROMPT_COUNT, PROMPT_LENGTH, KEY_VALUE_HEADS * HEAD_SIZE), 1.0, 6.0, ((0, 8), (1, 16)))
    resid = noise(key_of[5], (PROMPT_COUNT, RESPONSE_COUNT, RESPONSE_LENGTH, D), 1.0, 6.0, ((0, 8), (1, 16)))
    out_proj = noise(key_of[6], (QUERY_HEADS * HEAD_SIZE, D), (QUERY_HEADS * HEAD_SIZE) ** -0.5, 0.125, ((0, 8),))
    router = noise(key_of[7], (D, EXPERTS), D ** -0.5, 0.125)
    norm_gain = jnp.clip(1.0 + 0.18 * jax.random.normal(key_of[8], (D,), jnp.float32), 0.1, 1.9)
    w_gate = noise(key_of[9], (EXPERTS, D, FF), D ** -0.5, 0.125, ((0, 128),))
    w_up = noise(key_of[10], (EXPERTS, D, FF), D ** -0.5, 0.125, ((0, 128),))
    w_down = noise(key_of[11], (EXPERTS, FF, D), FF ** -0.5, 0.21875, ((0, 128),))
    expert_ids_keys = jax.random.split(jax.random.fold_in(key_of[12], 1), PROMPT_COUNT * RESPONSE_COUNT * RESPONSE_LENGTH // (RESP_DEV * RESPONSE_LENGTH))
    expert_ids_turns = jax.random.permutation(jax.random.fold_in(key_of[12], 3), PROMPT_COUNT * RESPONSE_COUNT * RESPONSE_LENGTH // (RESP_DEV * RESPONSE_LENGTH))
    expert_ids = jax.vmap(lambda own, number: assign_block(jax.random.fold_in(key_of[12], 2), own, number, RESP_DEV * RESPONSE_LENGTH, EXPERTS, TOPK, CAP, 2))(expert_ids_keys, expert_ids_turns).reshape((PROMPT_COUNT, RESPONSE_COUNT, RESPONSE_LENGTH, TOPK))
    lengths = draw_lengths(jax.random.fold_in(key_of[15], 71), 0)
    out_grad = noise(key_of[14], (PROMPT_COUNT, RESPONSE_COUNT, RESPONSE_LENGTH, D), 1.0, 6.0, ((0, 8), (1, 16)))
    return {"queries": queries, "response_keys": response_keys, "response_values": response_values, "prefix_keys": prefix_keys, "prompt_values": prompt_values, "resid": resid, "out_proj": out_proj, "router": router, "norm_gain": norm_gain, "w_gate": w_gate, "w_up": w_up, "w_down": w_down, "expert_ids": expert_ids, "lengths": lengths, "out_grad": out_grad}


def silu_parts(pre_gate):
    sigmoid = jax.nn.sigmoid(pre_gate)
    return (pre_gate * sigmoid, sigmoid * (1.0 + pre_gate * (1.0 - sigmoid)))

def allowed_keys(span_length, prompt_prefix):
    row_pos = jnp.arange(span_length)[:, None]
    col_pos = jnp.arange(prompt_prefix + span_length)[None, :]
    return (col_pos < prompt_prefix) | (col_pos - prompt_prefix <= row_pos)

def prompt_attention(query_matrix, key_matrix, value_matrix, prompt_key_rows, prompt_value_rows):
    item_count = query_matrix.shape[0]
    span_length = query_matrix.shape[1]
    prompt_prefix = prompt_key_rows.shape[0]
    group_index = QUERY_HEADS // KEY_VALUE_HEADS
    query_quintet = query_matrix.reshape(item_count, span_length, KEY_VALUE_HEADS, group_index, HEAD_SIZE)
    joined_keys = jnp.concatenate([jnp.broadcast_to(prompt_key_rows.reshape(1, prompt_prefix, KEY_VALUE_HEADS, HEAD_SIZE), (item_count, prompt_prefix, KEY_VALUE_HEADS, HEAD_SIZE)), key_matrix.reshape(item_count, span_length, KEY_VALUE_HEADS, HEAD_SIZE)], axis=1)
    joined_values = jnp.concatenate([jnp.broadcast_to(prompt_value_rows.reshape(1, prompt_prefix, KEY_VALUE_HEADS, HEAD_SIZE), (item_count, prompt_prefix, KEY_VALUE_HEADS, HEAD_SIZE)), value_matrix.reshape(item_count, span_length, KEY_VALUE_HEADS, HEAD_SIZE)], axis=1)
    scores = jnp.einsum('blkgd,bskd->bkgls', query_quintet.astype(jnp.float32), joined_keys.astype(jnp.float32)) * HEAD_SIZE ** (-0.5)
    scores = jnp.where(allowed_keys(span_length, prompt_prefix), scores, -jnp.inf)
    attn_probs = jax.nn.softmax(scores, axis=-1)
    probs_low = attn_probs.astype(jnp.bfloat16)
    attn_out = jnp.einsum('bkgls,bskd->blkgd', probs_low.astype(jnp.float32), joined_values.astype(jnp.float32)).astype(jnp.bfloat16)
    return (query_quintet, joined_keys, joined_values, attn_probs, probs_low, attn_out.reshape(item_count, span_length, QUERY_HEADS * HEAD_SIZE))

def attention_back(query_quintet, joined_keys, joined_values, attn_probs, probs_low, attention_gradient):
    item_count = query_quintet.shape[0]
    span_length = query_quintet.shape[1]
    gradient_quintet = attention_gradient.reshape(item_count, span_length, KEY_VALUE_HEADS, QUERY_HEADS // KEY_VALUE_HEADS, HEAD_SIZE)
    prob_back = jnp.einsum('blkgd,bskd->bkgls', gradient_quintet.astype(jnp.float32), joined_values.astype(jnp.float32))
    delta = lax.optimization_barrier(jnp.sum(attn_probs * prob_back, axis=-1, keepdims=True))
    score_back = (attn_probs * (prob_back - delta) * HEAD_SIZE ** (-0.5)).astype(jnp.bfloat16)
    query_grad = jnp.einsum('bkgls,bskd->blkgd', score_back.astype(jnp.float32), joined_keys.astype(jnp.float32)).astype(jnp.bfloat16)
    key_gradient = jnp.einsum('bkgls,blkgd->bskd', score_back.astype(jnp.float32), query_quintet.astype(jnp.float32))
    value_gradient = jnp.einsum('bkgls,blkgd->bskd', probs_low.astype(jnp.float32), gradient_quintet.astype(jnp.float32))
    return (query_grad.reshape(item_count, span_length, QUERY_HEADS * HEAD_SIZE), key_gradient, value_gradient)

def reference(queries, response_keys, response_values, prefix_keys, prompt_values, resid, out_proj, router, norm_gain, w_gate, w_up, w_down, expert_ids, lengths, out_grad):
    devices = PROMPT_COUNT * N_RESP
    dev_rows = RESP_DEV * RESPONSE_LENGTH
    copies = dev_rows * TOPK
    total_rows = devices * dev_rows
    contract_one = (((1,), (1,)), ((), ()))
    contract_zero = (((0,), (0,)), ((), ()))

    def attention_forward(items):
        return prompt_attention(*items)[5]
    attn = lax.map(attention_forward, (queries, response_keys, response_values, prefix_keys, prompt_values))
    attn_flat = attn.reshape(total_rows, QUERY_HEADS * HEAD_SIZE)
    xmid = resid.reshape(total_rows, D).astype(jnp.float32) + jnp.dot(attn_flat, out_proj, preferred_element_type=jnp.float32)
    rinv = lax.rsqrt(lax.optimization_barrier(jnp.mean(xmid * xmid, axis=-1, keepdims=True)) + 1e-06)
    normed = xmid * rinv
    hidden = (normed * norm_gain).astype(jnp.bfloat16)
    logits = jnp.dot(hidden, router, preferred_element_type=jnp.float32)
    ids = expert_ids.reshape(total_rows, TOPK)
    chosen = jnp.exp(jnp.take_along_axis(logits, ids, axis=1))
    gates = chosen / lax.optimization_barrier(jnp.sum(chosen, axis=1, keepdims=True))
    ids_dev = ids.reshape(devices, copies)

    def slots_of(block):
        onehot = (block[:, None] == jnp.arange(EXPERTS, dtype=jnp.int32)[None, :]).astype(jnp.int32)
        return lax.optimization_barrier(jnp.sum(jnp.cumsum(onehot, axis=0) * onehot, axis=1)) - 1
    slot = lax.map(slots_of, ids_dev).astype(jnp.int32)
    dev_index = jnp.arange(devices, dtype=jnp.int32)
    dev_grid = jnp.broadcast_to(dev_index[:, None], (devices, copies))
    copy_grid = jnp.broadcast_to(jnp.arange(copies, dtype=jnp.int32)[None, :], (devices, copies))
    table = jnp.full((EXPERTS, devices, CAP), copies, jnp.int32).at[ids_dev, dev_grid, slot].set(copy_grid)
    hidden_pad = jnp.concatenate([hidden.reshape(devices, dev_rows, D), jnp.zeros((devices, 1, D), jnp.bfloat16)], axis=1)
    flat_slot = (dev_grid * CAP + slot).astype(jnp.int32)

    def expert_forward(items):
        table_e, gate_e, up_e, down_e = items
        inputs = hidden_pad[dev_index[:, None], table_e // TOPK].reshape(devices * CAP, D)
        pre_gate = jnp.dot(inputs, gate_e, preferred_element_type=jnp.float32)
        pre_up = jnp.dot(inputs, up_e, preferred_element_type=jnp.float32)
        act = (silu_parts(pre_gate)[0] * pre_up).astype(jnp.bfloat16)
        return jnp.dot(act, down_e, preferred_element_type=jnp.float32).astype(jnp.bfloat16)
    expert_out = lax.map(expert_forward, (table, w_gate, w_up, w_down))
    out_copies = expert_out[ids_dev, flat_slot].reshape(total_rows, TOPK, D)
    layer_out = (xmid + lax.optimization_barrier(jnp.sum(gates[:, :, None] * out_copies.astype(jnp.float32), axis=1))).astype(jnp.bfloat16)
    live = (jnp.arange(RESPONSE_LENGTH, dtype=jnp.int32)[None, None, :] < lengths[:, :, None]).reshape(total_rows, 1)
    grad = jnp.where(live, out_grad.reshape(total_rows, D).astype(jnp.float32), 0.0)
    copy_grad = (gates[:, :, None] * grad[:, None, :]).astype(jnp.bfloat16)
    gate_back = jnp.einsum('rd,rkd->rk', grad, out_copies.astype(jnp.float32))
    grad_pad = jnp.concatenate([copy_grad.reshape(devices, copies, D), jnp.zeros((devices, 1, D), jnp.bfloat16)], axis=1)

    def expert_backward(items):
        table_e, gate_e, up_e, down_e = items
        inputs = hidden_pad[dev_index[:, None], table_e // TOPK].reshape(devices * CAP, D)
        pre_gate = jnp.dot(inputs, gate_e, preferred_element_type=jnp.float32)
        pre_up = jnp.dot(inputs, up_e, preferred_element_type=jnp.float32)
        silu_value, silu_slope = silu_parts(pre_gate)
        act = (silu_value * pre_up).astype(jnp.bfloat16)
        out_back = grad_pad[dev_index[:, None], table_e].reshape(devices * CAP, D)
        act_back = lax.dot_general(out_back, down_e, contract_one, preferred_element_type=jnp.float32)
        down_part = lax.dot_general(act, out_back, contract_zero, preferred_element_type=jnp.float32).astype(jnp.bfloat16)
        pre_back = (act_back * pre_up * silu_slope).astype(jnp.bfloat16)
        up_back = (act_back * silu_value).astype(jnp.bfloat16)
        gate_part = lax.dot_general(inputs, pre_back, contract_zero, preferred_element_type=jnp.float32).astype(jnp.bfloat16)
        up_part = lax.dot_general(inputs, up_back, contract_zero, preferred_element_type=jnp.float32).astype(jnp.bfloat16)
        input_back = (lax.dot_general(pre_back, gate_e, contract_one, preferred_element_type=jnp.float32) + lax.dot_general(up_back, up_e, contract_one, preferred_element_type=jnp.float32)).astype(jnp.bfloat16)
        return (input_back, gate_part, up_part, down_part)
    input_back, gate_grad, up_grad, down_grad = lax.map(expert_backward, (table, w_gate, w_up, w_down))
    back_copies = input_back[ids_dev, flat_slot].reshape(total_rows, TOPK, D)
    hidden_back = lax.optimization_barrier(jnp.sum(back_copies.astype(jnp.float32), axis=1))
    route_back = gates * (gate_back - lax.optimization_barrier(jnp.sum(gates * gate_back, axis=1, keepdims=True)))
    picked = ids[:, :, None] == jnp.arange(EXPERTS, dtype=jnp.int32)[None, None, :]
    logit_back = lax.optimization_barrier(jnp.sum(jnp.where(picked, route_back[:, :, None], 0.0), axis=1)).astype(jnp.bfloat16)
    router_grad = lax.dot_general(hidden, logit_back, contract_zero, preferred_element_type=jnp.float32)
    hidden_back = hidden_back + lax.dot_general(logit_back, router, contract_one, preferred_element_type=jnp.float32)
    gain_grad = lax.optimization_barrier(jnp.sum(hidden_back * normed, axis=0))
    norm_back = hidden_back * norm_gain
    xmid_back = grad + rinv * (norm_back - normed * lax.optimization_barrier(jnp.mean(norm_back * normed, axis=-1, keepdims=True)))
    resid_grad = xmid_back.astype(jnp.bfloat16)
    attention_gradient = lax.dot_general(resid_grad, out_proj, contract_one, preferred_element_type=jnp.float32).astype(jnp.bfloat16)

    def attention_backward(items):
        query_matrix, key_matrix, value_matrix, prompt_key_rows, prompt_value_rows, back_rows = items
        query_quintet, joined_keys, joined_values, attn_probs, probs_low, unused_out = prompt_attention(query_matrix, key_matrix, value_matrix, prompt_key_rows, prompt_value_rows)
        query_grad, key_gradient, value_gradient = attention_back(query_quintet, joined_keys, joined_values, attn_probs, probs_low, back_rows)
        prompt_prefix = prompt_key_rows.shape[0]
        prompt_key_gradient = lax.optimization_barrier(jnp.sum(key_gradient[:, :prompt_prefix], axis=0)).astype(jnp.bfloat16).reshape(prompt_prefix, KEY_VALUE_HEADS * HEAD_SIZE)
        prompt_value_gradient = lax.optimization_barrier(jnp.sum(value_gradient[:, :prompt_prefix], axis=0)).astype(jnp.bfloat16).reshape(prompt_prefix, KEY_VALUE_HEADS * HEAD_SIZE)
        local_key_gradient = key_gradient[:, prompt_prefix:].astype(jnp.bfloat16).reshape(RESPONSE_COUNT, RESPONSE_LENGTH, KEY_VALUE_HEADS * HEAD_SIZE)
        local_value_gradient = value_gradient[:, prompt_prefix:].astype(jnp.bfloat16).reshape(RESPONSE_COUNT, RESPONSE_LENGTH, KEY_VALUE_HEADS * HEAD_SIZE)
        return (query_grad, local_key_gradient, local_value_gradient, prompt_key_gradient, prompt_value_gradient)
    query_grad, resp_key_grad, resp_value_grad, prefix_key_grad, prefix_value_grad = lax.map(attention_backward, (queries, response_keys, response_values, prefix_keys, prompt_values, attention_gradient.reshape(PROMPT_COUNT, RESPONSE_COUNT, RESPONSE_LENGTH, QUERY_HEADS * HEAD_SIZE)))
    shape_rows = (PROMPT_COUNT, RESPONSE_COUNT, RESPONSE_LENGTH, D)
    return (layer_out.reshape(shape_rows), resid_grad.reshape(shape_rows), query_grad, resp_key_grad, resp_value_grad, prefix_key_grad, prefix_value_grad, router_grad, gain_grad, gate_grad, up_grad, down_grad)
```

```python
import jax
import jax.numpy as jnp
from jax import lax
from jax.experimental import pallas as pl
from jax.experimental.pallas import tpu as pltpu
from jax.sharding import PartitionSpec as P

D = 2048
HEADS = 16
KV = 2
GROUP = HEADS // KV
HS = 128
FF = 768
TOPK = 4
PREFIX = 512
SPAN = 64
ROWS = 128
EXPERTS = 128
CAP = 6
N_PROMPT = 8
N_RESP = 16
DEVICES = 128
SLOTS = DEVICES * CAP
PACKED = DEVICES * 8
MAIN = 1536
TAIL = 512
EXTRA = 128
SCALE = HS ** (-0.5)
BF = jnp.bfloat16
F32 = jnp.float32
MIB = 1024 * 1024


def mm(a, b):
    return jnp.dot(a, b, preferred_element_type=F32)


def mm_nt(a, b):
    return lax.dot_general(a, b, (((1,), (1,)), ((), ())), preferred_element_type=F32)


def mm_tn(a, b):
    return lax.dot_general(a, b, (((0,), (0,)), ((), ())), preferred_element_type=F32)


def iota(shape, dim):
    return lax.broadcasted_iota(jnp.int32, shape, dim)


def chosen_by_row(ids):
    lanes = iota((ROWS, EXPERTS), 1)
    hit = ids[:, 0:1] == lanes
    for k in range(1, TOPK):
        hit = hit | (ids[:, k : k + 1] == lanes)
    return hit


def chosen_by_expert(ids_t):
    subs = iota((EXPERTS, ROWS), 0)
    hit = ids_t[0:1, :] == subs
    for k in range(1, TOPK):
        hit = hit | (ids_t[k : k + 1, :] == subs)
    return hit


def to_bf(mask):
    return jnp.where(mask, 1.0, 0.0).astype(BF)


def packed_slots(ids_t):
    hit = chosen_by_expert(ids_t)
    before = to_bf(iota((ROWS, ROWS), 0) < iota((ROWS, ROWS), 1))
    slot = mm(to_bf(hit), before)
    slot = jnp.where(hit, slot, -1.0).astype(BF)
    spread = to_bf((iota((PACKED, EXPERTS), 0) >> 3) == iota((PACKED, EXPERTS), 1))
    return mm(spread, slot).astype(jnp.int32)


def packed_slots_by_row(ids):
    hit = chosen_by_row(ids)
    before = to_bf(iota((ROWS, ROWS), 1) < iota((ROWS, ROWS), 0))
    slot = mm(before, to_bf(hit))
    slot = jnp.where(hit, slot, -1.0).astype(BF)
    spread = to_bf(iota((EXPERTS, PACKED), 0) == (iota((EXPERTS, PACKED), 1) >> 3))
    return mm(slot, spread).astype(jnp.int32)


def selectors(slot, place):
    head = to_bf((slot == place) & (place < CAP))
    tails = [to_bf((slot == place * 3 - 18 + j) & (place >= CAP)) for j in range(3)]
    return head, tails


def pack_rows(rows, head, tails, out_ref):
    last = rows[:, MAIN:]
    for j in range(3):
        select = jnp.concatenate([head, tails[j]], axis=1)
        both = jnp.concatenate([rows[:, j * TAIL : (j + 1) * TAIL], last], axis=0)
        out_ref[:, j * TAIL : (j + 1) * TAIL] = mm(select, both).astype(BF)


def combine(head, tails, packed_ref):
    pieces = [mm(head, packed_ref[:, j * TAIL : (j + 1) * TAIL]) for j in range(3)]
    last = mm(tails[0], packed_ref[:, 0:TAIL])
    for j in range(1, 3):
        last = last + mm(tails[j], packed_ref[:, j * TAIL : (j + 1) * TAIL])
    return pieces + [last]


def static_selectors(by_slot):
    shape, slot_dim = ((96, 128), 0) if by_slot else ((128, 96), 1)
    slot = iota(shape, slot_dim)
    packed = iota(shape, 1 - slot_dim)
    place = packed & 7
    base = (packed >> 3) * CAP
    head = to_bf((slot == base + place) & (place < CAP))
    tails = [to_bf((slot == base + place * 3 - 18 + j) & (place >= CAP)) for j in range(3)]
    return head, tails


def grad_pack_kernel(ids_t_ref, ids_ref, live_ref, grad_ref, out_ref):
    slot = packed_slots(ids_t_ref[...])
    head, tails = selectors(slot, iota((PACKED, ROWS), 0) & 7)
    grad = jnp.where(live_ref[...] > 0, grad_ref[...].astype(F32), 0.0).astype(BF)
    pack_rows(grad, head, tails, out_ref)
    out_ref[:, MAIN:] = mm(head, to_bf(chosen_by_row(ids_ref[...]))).astype(BF)


def allowed_own():
    key = iota((ROWS, ROWS), 0)
    row = iota((ROWS, ROWS), 1)
    return ((key >> 6) == (row >> 6)) & ((key & 63) <= (row & 63))


def attention_kernel(q_ref, rk_ref, rv_ref, prefix_ref, out_ref, lse_ref):
    mask = allowed_own()
    for kv in range(KV):
        lanes = slice(kv * HS, (kv + 1) * HS)
        vlanes = slice((KV + kv) * HS, (KV + kv + 1) * HS)
        keys = jnp.concatenate([prefix_ref[:, lanes], rk_ref[:, lanes]], axis=0)
        values = jnp.concatenate([prefix_ref[:, vlanes], rv_ref[:, lanes]], axis=0)
        values_t = values.astype(F32).T.astype(BF)
        for g in range(GROUP):
            h = kv * GROUP + g
            cols = slice(h * HS, (h + 1) * HS)
            scores = mm_nt(keys, q_ref[:, cols]) * SCALE
            near = jnp.where(mask, scores[PREFIX:], -1e30)
            scores = jnp.concatenate([scores[:PREFIX], near], axis=0)
            top = jnp.max(scores, axis=0, keepdims=True)
            probs = jnp.exp(scores - top)
            total = jnp.sum(probs, axis=0, keepdims=True)
            low = (probs * (1.0 / total)).astype(BF)
            out_ref[:, cols] = mm(values_t, low).T.astype(BF)
            lse_ref[h : h + 1, :] = top + jnp.log(total)


def project_kernel(
    core_ref, attn_ref, attn_other_ref, w_ref, w_other_ref, resid_ref, gain_ref, router_ref, ids_ref, ids_t_ref, xmid_ref, hidden_ref, gates_ref, out_ref
):
    step = pl.program_id(0)
    attn = jnp.concatenate([attn_ref[...], attn_other_ref[...]], axis=1)
    part = mm(attn, jnp.concatenate([w_ref[...], w_other_ref[...]], axis=0))

    @pl.when(step == 0)
    def _():
        xmid_ref[...] = resid_ref[...].astype(F32) + part

    @pl.when(step > 0)
    def _():
        xmid_ref[...] += part

    @pl.when(step == pl.num_programs(0) - 1)
    def _():
        xmid = xmid_ref[...]
        rinv = lax.rsqrt(jnp.mean(xmid * xmid, axis=-1, keepdims=True) + 1e-06)
        hidden = (xmid * rinv * gain_ref[...]).astype(BF)
        hidden_ref[...] = hidden
        slot = packed_slots(ids_t_ref[...])
        head, tails = selectors(slot, iota((PACKED, ROWS), 0) & 7)
        pack_rows(hidden, head, tails, out_ref)
        logits = mm(hidden, router_ref[...])
        chosen = jnp.where(chosen_by_row(ids_ref[...]), jnp.exp(logits), 0.0)
        gates_ref[...] = chosen / jnp.sum(chosen, axis=1, keepdims=True)


def expert_kernel(
    own_ref, router_ref, x_ref, g_ref, wg_hbm, wu_hbm, wd_hbm,
    back_hbm, out_hbm, xc_hbm, ob_hbm, act_hbm, pb_hbm, ub_hbm,
    wg, wu, wd, xc, ob, act, pb, ub, pg, pu, outs, back8, out8, in_sem, out_sem,
):
    copies = [
        pltpu.make_async_copy(src, dst, in_sem.at[i])
        for i, (src, dst) in enumerate(((wg_hbm, wg), (wu_hbm, wu), (wd_hbm, wd)))
    ]
    for copy in copies:
        copy.start()
    stores = [
        pltpu.make_async_copy(src, dst, out_sem.at[i])
        for i, (src, dst) in enumerate(
            ((xc, xc_hbm), (act, act_hbm), (ob, ob_hbm), (out8, out_hbm), (pb, pb_hbm), (ub, ub_hbm), (back8, back_hbm))
        )
    ]

    head, tails = static_selectors(True)
    tail3 = jnp.concatenate(tails, axis=1)

    def unpack(block, src, dst):
        rows = pl.ds(pl.multiple_of(block * 128, 128), 128)
        to = pl.ds(pl.multiple_of(block * 96, 32), 96)
        part = src[rows, 0:MAIN]
        dst[to, 0:MAIN] = mm(head, part).astype(BF)
        stacked = jnp.concatenate([part[:, j * TAIL : (j + 1) * TAIL] for j in range(3)], axis=0)
        dst[to, MAIN:] = mm(tail3, stacked).astype(BF)

    @pl.loop(0, 8)
    def _(block):
        unpack(block, x_ref, xc)

    stores[0].start()
    copies[0].wait()
    copies[1].wait()

    @pl.loop(0, 3)
    def _(n):
        cols = pl.ds(pl.multiple_of(n * 256, 256), 256)
        gate = mm(xc[...], wg[:, cols])
        up = mm(xc[...], wu[:, cols])
        pg[:, cols] = gate
        pu[:, cols] = up
        act[:, cols] = (gate * jax.nn.sigmoid(gate) * up).astype(BF)

    stores[1].start()

    @pl.loop(0, 8)
    def _(block):
        unpack(block, g_ref, ob)

    mask = jnp.concatenate([mm(head, g_ref[i * 128 : (i + 1) * 128, MAIN:]) for i in range(8)], axis=0)
    own_hi = own_ref[0:1, :]
    own_lo = own_ref[1:2, :]
    logits = mm(xc[...], router_ref[...])
    chosen = jnp.where(mask > 0.5, jnp.exp(logits), 0.0)
    total = jnp.sum(chosen, axis=1, keepdims=True)
    own = jnp.sum(chosen * own_hi, axis=1, keepdims=True)
    gate_col = jnp.where(total > 0.0, own / jnp.where(total > 0.0, total, 1.0), 0.0)

    copies[2].wait()

    def out_tile(n, gate_back):
        cols = pl.ds(pl.multiple_of(n * 256, 256), 256)
        value = mm(act[...], wd[:, cols]).astype(BF).astype(F32)
        raw = ob[:, cols].astype(F32)
        outs[:, cols] = (gate_col * value).astype(BF)
        ob[:, cols] = (gate_col * raw).astype(BF)
        both = value * raw
        return gate_back + both[:, 0:128] + both[:, 128:256]

    gate_back = lax.fori_loop(0, 8, out_tile, jnp.zeros((SLOTS, 128), F32))
    stores[2].start()
    gate_back = jnp.sum(gate_back, axis=1, keepdims=True)
    back_hi = gate_back.astype(BF).astype(F32)
    extra = (back_hi * own_hi + (gate_back - back_hi) * own_lo).astype(BF)

    @pl.loop(0, 3)
    def _(n):
        cols = pl.ds(pl.multiple_of(n * 256, 256), 256)
        act_back = mm_nt(ob[...], wd[cols, :])
        gate = pg[:, cols]
        sig = jax.nn.sigmoid(gate)
        pb[:, cols] = (act_back * pu[:, cols] * (sig * (1.0 + gate * (1.0 - sig)))).astype(BF)
        ub[:, cols] = (act_back * (gate * sig)).astype(BF)

    stores[4].start()
    stores[5].start()

    head_t, tails_t = static_selectors(False)
    selects = [jnp.concatenate([head_t, tail], axis=1) for tail in tails_t]

    def pack(block, src, dst):
        rows = pl.ds(pl.multiple_of(block * 128, 128), 128)
        at = pl.ds(pl.multiple_of(block * 96, 32), 96)
        last = src[at, MAIN:]
        for j in range(3):
            both = jnp.concatenate([src[at, j * TAIL : (j + 1) * TAIL], last], axis=0)
            dst[rows, j * TAIL : (j + 1) * TAIL] = mm(selects[j], both).astype(BF)

    @pl.loop(0, 8)
    def _(block):
        pack(block, outs, out8)

    stores[3].start()

    @pl.loop(0, 8)
    def _(n):
        cols = pl.ds(pl.multiple_of(n * 256, 256), 256)
        outs[:, cols] = (mm_nt(pb[...], wg[cols, :]) + mm_nt(ub[...], wu[cols, :])).astype(BF)

    @pl.loop(0, 8)
    def _(block):
        pack(block, outs, back8)

    for i in range(8):
        back8[i * 128 : (i + 1) * 128, MAIN:] = mm(head_t, extra[i * 96 : (i + 1) * 96]).astype(BF)
    stores[6].start()
    for store in stores:
        store.wait()


def weight_grad_kernel(xc_ref, ob_ref, act_ref, pb_ref, ub_ref, gate_ref, up_ref, down_ref, act_t):
    @pl.when(pl.program_id(0) == 0)
    def _():
        act_t[...] = act_ref[...].astype(F32).T.astype(BF)

    xt = xc_ref[...].astype(F32).T.astype(BF)
    gate_ref[...] = mm(xt, pb_ref[...]).astype(BF)
    up_ref[...] = mm(xt, ub_ref[...]).astype(BF)
    down_ref[...] = mm(act_t[...], ob_ref[...]).astype(BF)


def back_kernel(
    core_ref, back_ref, xmid_ref, hidden_ref, gates_ref, grad_ref, live_ref, ids_ref, gain_ref, router_ref, w_ref, w_other_ref,
    resid_ref, sums_ref, attn_back_ref, acc,
):
    @pl.when(pl.program_id(0) == 0)
    def _():
        slot = packed_slots_by_row(ids_ref[...])
        head, tails = selectors(slot, iota((ROWS, PACKED), 1) & 7)
        pieces = combine(head, tails, back_ref)
        expert = iota((PACKED, EXPERTS), 0) >> 3
        lane = iota((PACKED, EXPERTS), 1)
        extra = back_ref[:, MAIN:].astype(F32)
        hi = mm(head, jnp.where(lane == expert, extra, 0.0).astype(BF))
        lo = mm(head, jnp.where(lane == ((expert + 64) & 127), extra, 0.0).astype(BF))
        gate_back = hi + pltpu.roll(lo, 64, 1)
        gates = gates_ref[...]
        route = gates * (gate_back - jnp.sum(gates * gate_back, axis=1, keepdims=True))
        logit_back = route.astype(BF)
        sums_ref[:, 0:EXPERTS] = mm_tn(hidden_ref[...], logit_back).astype(BF)
        xmid = xmid_ref[...]
        rinv = lax.rsqrt(jnp.mean(xmid * xmid, axis=-1, keepdims=True) + 1e-06)
        ones = jnp.ones((ROWS, EXPERTS), BF)
        mean = jnp.zeros((ROWS, 1), F32)
        for j in range(4):
            cols = slice(j * TAIL, (j + 1) * TAIL)
            value = pieces[j] + mm_nt(logit_back, router_ref[cols, :])
            normed = xmid[:, cols] * rinv
            sums_ref[cols, EXPERTS:] = mm_tn((value * normed).astype(BF), ones).astype(BF)
            value = value * gain_ref[:, cols]
            acc[:, cols] = value
            mean = mean + jnp.sum(value * normed, axis=-1, keepdims=True)
        mean = mean * (1.0 / D)
        grad = jnp.where(live_ref[...] > 0, grad_ref[...].astype(F32), 0.0)
        resid_ref[...] = (grad + rinv * (acc[...] - xmid * rinv * mean)).astype(BF)

    first = core_ref[0] == 0
    near, far = w_ref[...], w_other_ref[...]
    half = near.shape[0]
    value = mm_nt(resid_ref[...], jnp.concatenate([near, far], axis=0)).astype(BF)

    @pl.when(first)
    def _():
        attn_back_ref[...] = value

    @pl.when(jnp.logical_not(first))
    def _():
        attn_back_ref[:, 0:half] = value[:, half:]
        attn_back_ref[:, half:] = value[:, 0:half]


def attention_back_kernel(q_ref, rk_ref, rv_ref, prefix_ref, lse_ref, ab_ref, dq_ref, dk_ref, dv_ref, dprefix_ref, ds_all, p_all):
    mask = allowed_own()
    for kv in range(KV):
        lanes = slice(kv * HS, (kv + 1) * HS)
        vlanes = slice((KV + kv) * HS, (KV + kv + 1) * HS)
        keys = jnp.concatenate([prefix_ref[:, lanes], rk_ref[:, lanes]], axis=0)
        values = jnp.concatenate([prefix_ref[:, vlanes], rv_ref[:, lanes]], axis=0)
        keys_t = keys.astype(F32).T.astype(BF)
        q_parts = []
        ab_parts = []
        for g in range(GROUP):
            h = kv * GROUP + g
            cols = slice(h * HS, (h + 1) * HS)
            q = q_ref[:, cols]
            ab = ab_ref[:, cols]
            q_parts.append(q)
            ab_parts.append(ab)
            scores = mm_nt(keys, q) * SCALE
            near = jnp.where(mask, scores[PREFIX:], -1e30)
            scores = jnp.concatenate([scores[:PREFIX], near], axis=0)
            probs = jnp.exp(scores - lse_ref[h : h + 1, :])
            prob_back = mm_nt(values, ab)
            delta = jnp.sum(probs * prob_back, axis=0, keepdims=True)
            score_back = (probs * (prob_back - delta) * SCALE).astype(BF)
            at = slice(g * ROWS, (g + 1) * ROWS)
            p_all[:, at] = probs.astype(BF)
            ds_all[:, at] = score_back
            dq_ref[:, cols] = mm(keys_t, score_back).T.astype(BF)
        dk = mm(ds_all[...], jnp.concatenate(q_parts, axis=0)).astype(BF)
        dv = mm(p_all[...], jnp.concatenate(ab_parts, axis=0)).astype(BF)
        dprefix_ref[:, lanes] = dk[:PREFIX]
        dprefix_ref[:, vlanes] = dv[:PREFIX]
        dk_ref[:, lanes] = dk[PREFIX:]
        dv_ref[:, lanes] = dv[PREFIX:]


def layer_out_kernel(out8_ref, xmid_ref, ids_ref, out_ref):
    slot = packed_slots_by_row(ids_ref[...])
    head, tails = selectors(slot, iota((ROWS, PACKED), 1) & 7)
    pieces = combine(head, tails, out8_ref)
    for j in range(4):
        cols = slice(j * TAIL, (j + 1) * TAIL)
        out_ref[:, cols] = (xmid_ref[:, cols] + pieces[j]).astype(BF)


def struct(shape, dtype):
    return jax.ShapeDtypeStruct(shape, dtype)


def params(limit):
    return pltpu.CompilerParams(vmem_limit_bytes=limit * MIB)


def cost(flops, moved):
    return pl.CostEstimate(flops=int(flops), bytes_accessed=int(moved), transcendentals=0)


VMEM_SPEC = pl.BlockSpec(memory_space=pltpu.VMEM)
ANY_SPEC = pl.BlockSpec(memory_space=pl.ANY)


def whole(shape):
    return pl.BlockSpec(shape, lambda *at: (0,) * len(shape))


def exchange(block, width):
    moved = lax.all_to_all(
        block.reshape(DEVICES, 8, width), ("prompt", "resp"), split_axis=0, concat_axis=0, tiled=True
    )
    return moved.reshape(PACKED, width)


def shards(
    queries, response_keys, response_values, prefix_keys, prompt_values, resid, out_proj, router, norm_gain,
    w_gate, w_up, w_down, expert_ids, lengths, out_grad,
):
    p_at = lax.axis_index("prompt")
    r_at = lax.axis_index("resp")
    me = p_at * N_RESP + r_at
    lane = jnp.arange(EXPERTS, dtype=jnp.int32)
    own = jnp.stack([lane == me] + [lane == (me + 64) % EXPERTS] * 7).astype(F32)
    ids = expert_ids.reshape(ROWS, TOPK)
    ids_t = ids.T
    live = (jnp.arange(SPAN, dtype=jnp.int32)[None, :] < lengths[0][:, None]).astype(F32).reshape(ROWS, 1)
    grad = out_grad.reshape(ROWS, D)
    q = queries.reshape(ROWS, D)
    rk = response_keys.reshape(ROWS, KV * HS)
    rv = response_values.reshape(ROWS, KV * HS)
    gain = norm_gain.reshape(1, D)

    prefix_part = jnp.concatenate([prefix_keys[0], prompt_values[0]], axis=1)
    prefix = lax.all_to_all(
        jnp.broadcast_to(prefix_part[None], (N_RESP,) + prefix_part.shape), "resp", split_axis=0, concat_axis=0, tiled=True
    ).reshape(PREFIX, 2 * KV * HS)
    piece = D // DEVICES
    half = D // N_PROMPT // 2
    core = r_at % 2
    w_own = lax.dynamic_slice(out_proj, (core * half, 0), (half, D))
    w_own = lax.all_gather(w_own, "prompt", axis=0, tiled=True)
    w_other = lax.ppermute(w_own, "resp", [(i, i ^ 1) for i in range(N_RESP)])
    core = core.astype(jnp.int32).reshape(1)

    grad8 = pl.pallas_call(
        grad_pack_kernel,
        out_shape=struct((PACKED, MAIN + EXTRA), BF),
        in_specs=[VMEM_SPEC] * 4,
        out_specs=VMEM_SPEC,
        compiler_params=params(32),
        cost_estimate=cost(1.2e9, 4e6),
        name="grad_pack",
    )(ids_t, ids, live, grad)
    grad8 = exchange(grad8, MAIN + EXTRA)

    attn, lse = pl.pallas_call(
        attention_kernel,
        out_shape=(struct((ROWS, D), BF), struct((HEADS, ROWS), F32)),
        in_specs=[VMEM_SPEC] * 4,
        out_specs=(VMEM_SPEC, VMEM_SPEC),
        compiler_params=params(32),
        cost_estimate=cost(4e9, 2e6),
        name="attention",
    )(q, rk, rv, prefix)

    steps = N_PROMPT
    xmid, hidden, gates, x8 = pl.pallas_call(
        project_kernel,
        grid_spec=pltpu.PrefetchScalarGridSpec(
            num_scalar_prefetch=1,
            grid=(steps,),
            in_specs=[
                pl.BlockSpec((ROWS, half), lambda i, c: (0, 2 * i + c[0])),
                pl.BlockSpec((ROWS, half), lambda i, c: (0, 2 * i + 1 - c[0])),
                pl.BlockSpec((half, D), lambda i, c: (i, 0)),
                pl.BlockSpec((half, D), lambda i, c: (i, 0)),
                whole((ROWS, D)), whole((1, D)), whole((D, EXPERTS)), whole((ROWS, TOPK)), whole((TOPK, ROWS)),
            ],
            out_specs=(whole((ROWS, D)), whole((ROWS, D)), whole((ROWS, EXPERTS)), whole((PACKED, MAIN))),
        ),
        out_shape=(
            struct((ROWS, D), F32), struct((ROWS, D), BF), struct((ROWS, EXPERTS), F32), struct((PACKED, MAIN), BF)
        ),
        compiler_params=params(40),
        cost_estimate=cost(3e9, 14e6),
        name="project",
    )(core, attn, attn, w_own, w_other, resid.reshape(ROWS, D), gain, router, ids, ids_t)
    x8 = exchange(x8, MAIN)

    back8, out8, xc, ob, act, pb, ub = pl.pallas_call(
        expert_kernel,
        out_shape=(
            struct((PACKED, MAIN + EXTRA), BF), struct((PACKED, MAIN), BF), struct((SLOTS, D), BF),
            struct((SLOTS, D), BF), struct((SLOTS, FF), BF), struct((SLOTS, FF), BF), struct((SLOTS, FF), BF),
        ),
        in_specs=[VMEM_SPEC] * 4 + [ANY_SPEC] * 3,
        out_specs=(ANY_SPEC,) * 7,
        scratch_shapes=[
            pltpu.VMEM((D, FF), BF), pltpu.VMEM((D, FF), BF), pltpu.VMEM((FF, D), BF),
            pltpu.VMEM((SLOTS, D), BF), pltpu.VMEM((SLOTS, D), BF),
            pltpu.VMEM((SLOTS, FF), BF), pltpu.VMEM((SLOTS, FF), BF), pltpu.VMEM((SLOTS, FF), BF),
            pltpu.VMEM((SLOTS, FF), F32), pltpu.VMEM((SLOTS, FF), F32),
            pltpu.VMEM((SLOTS, D), BF), pltpu.VMEM((PACKED, MAIN + EXTRA), BF), pltpu.VMEM((PACKED, MAIN), BF),
            pltpu.SemaphoreType.DMA((3,)), pltpu.SemaphoreType.DMA((7,)),
        ],
        compiler_params=params(58),
        cost_estimate=cost(16e9, 32e6),
        name="expert",
    )(own, router, x8, grad8, w_gate[0], w_up[0], w_down[0])
    back8 = exchange(back8, MAIN + EXTRA)
    out8 = exchange(out8, MAIN)

    gate_grad, up_grad, down_grad = pl.pallas_call(
        weight_grad_kernel,
        grid=(8,),
        out_shape=(struct((D, FF), BF), struct((D, FF), BF), struct((FF, D), BF)),
        in_specs=[
            pl.BlockSpec((SLOTS, 256), lambda i: (0, i)), pl.BlockSpec((SLOTS, 256), lambda i: (0, i)),
            whole((SLOTS, FF)), whole((SLOTS, FF)), whole((SLOTS, FF)),
        ],
        out_specs=(
            pl.BlockSpec((256, FF), lambda i: (i, 0)), pl.BlockSpec((256, FF), lambda i: (i, 0)),
            pl.BlockSpec((FF, 256), lambda i: (0, i)),
        ),
        scratch_shapes=[pltpu.VMEM((FF, SLOTS), BF)],
        compiler_params=params(32),
        cost_estimate=cost(7.3e9, 20e6),
        name="weight_grad",
    )(xc, ob, act, pb, ub)

    resid_grad, sums, attn_back = pl.pallas_call(
        back_kernel,
        grid_spec=pltpu.PrefetchScalarGridSpec(
            num_scalar_prefetch=1,
            grid=(steps,),
            in_specs=[
                whole((PACKED, MAIN + EXTRA)), whole((ROWS, D)), whole((ROWS, D)), whole((ROWS, EXPERTS)),
                whole((ROWS, D)), whole((ROWS, 1)), whole((ROWS, TOPK)), whole((1, D)), whole((D, EXPERTS)),
                pl.BlockSpec((half, D), lambda i, c: (i, 0)),
                pl.BlockSpec((half, D), lambda i, c: (i, 0)),
            ],
            out_specs=(
                whole((ROWS, D)), whole((D, 2 * EXPERTS)), pl.BlockSpec((ROWS, 2 * half), lambda i, c: (0, i))
            ),
            scratch_shapes=[pltpu.VMEM((ROWS, D), F32)],
        ),
        out_shape=(struct((ROWS, D), BF), struct((D, 2 * EXPERTS), BF), struct((ROWS, D), BF)),
        compiler_params=params(48),
        cost_estimate=cost(3e9, 16e6),
        name="back",
    )(core, back8, xmid, hidden, gates, grad, live, ids, gain, router, w_own, w_other)

    query_grad, resp_key_grad, resp_value_grad, prefix_grad = pl.pallas_call(
        attention_back_kernel,
        out_shape=(
            struct((ROWS, D), BF), struct((ROWS, KV * HS), BF), struct((ROWS, KV * HS), BF),
            struct((PREFIX, 2 * KV * HS), BF),
        ),
        in_specs=[VMEM_SPEC] * 6,
        out_specs=(VMEM_SPEC,) * 4,
        scratch_shapes=[pltpu.VMEM((PREFIX + ROWS, GROUP * ROWS), BF)] * 2,
        compiler_params=params(32),
        cost_estimate=cost(8e9, 4e6),
        name="attention_back",
    )(q, rk, rv, prefix, lse, attn_back)

    prefix_grad = lax.all_to_all(
        prefix_grad.reshape(N_RESP, PREFIX // N_RESP, 2 * KV * HS), "resp", split_axis=0, concat_axis=0, tiled=True
    )
    prefix_grad = jnp.sum(prefix_grad.astype(F32), axis=0).astype(BF)

    sums = lax.all_to_all(
        sums.reshape(DEVICES, piece, 2 * EXPERTS), ("prompt", "resp"), split_axis=0, concat_axis=0, tiled=True
    )
    sums = jnp.sum(sums.astype(F32), axis=0).astype(BF)
    sums = lax.all_to_all(
        jnp.broadcast_to(sums[None], (DEVICES, piece, 2 * EXPERTS)),
        ("prompt", "resp"), split_axis=0, concat_axis=0, tiled=True,
    ).reshape(D, 2 * EXPERTS)

    layer_out = pl.pallas_call(
        layer_out_kernel,
        out_shape=struct((ROWS, D), BF),
        in_specs=[VMEM_SPEC] * 3,
        out_specs=VMEM_SPEC,
        compiler_params=params(32),
        cost_estimate=cost(1e9, 5e6),
        name="layer_out",
    )(out8, xmid, ids)

    rows_shape = (1, ROWS // SPAN, SPAN, D)
    near_shape = (1, ROWS // SPAN, SPAN, KV * HS)
    return (
        layer_out.reshape(rows_shape),
        resid_grad.reshape(rows_shape),
        query_grad.reshape(rows_shape),
        resp_key_grad.reshape(near_shape),
        resp_value_grad.reshape(near_shape),
        prefix_grad[None, :, : KV * HS],
        prefix_grad[None, :, KV * HS :],
        sums[:, :EXPERTS].astype(F32),
        sums[:, EXPERTS].astype(F32),
        gate_grad[None],
        up_grad[None],
        down_grad[None],
    )


def solution(mesh):
    in_specs = (
        P("prompt", "resp", None, None),
        P("prompt", "resp", None, None),
        P("prompt", "resp", None, None),
        P("prompt", "resp", None),
        P("prompt", "resp", None),
        P("prompt", "resp", None, None),
        P("prompt", None),
        P(),
        P(),
        P(("prompt", "resp"), None, None),
        P(("prompt", "resp"), None, None),
        P(("prompt", "resp"), None, None),
        P("prompt", "resp", None, None),
        P("prompt", "resp"),
        P("prompt", "resp", None, None),
    )
    out_specs = (
        P("prompt", "resp", None, None),
        P("prompt", "resp", None, None),
        P("prompt", "resp", None, None),
        P("prompt", "resp", None, None),
        P("prompt", "resp", None, None),
        P("prompt", "resp", None),
        P("prompt", "resp", None),
        P(),
        P(),
        P(("prompt", "resp"), None, None),
        P(("prompt", "resp"), None, None),
        P(("prompt", "resp"), None, None),
    )
    return jax.shard_map(shards, mesh=mesh, in_specs=in_specs, out_specs=out_specs, check_vma=False)
```

```python
import jax
import jax.numpy as jnp
from jax import lax
from jax.experimental import pallas as pl
from jax.experimental.pallas import tpu as pltpu
from jax.sharding import PartitionSpec as P

D = 2048
HEADS = 16
KV = 2
GROUP = HEADS // KV
HS = 128
FF = 768
TOPK = 4
PREFIX = 512
SPAN = 64
ROWS = 128
EXPERTS = 128
CAP = 6
N_PROMPT = 8
N_RESP = 16
DEVICES = 128
SLOTS = DEVICES * CAP
SHARE = PREFIX // N_RESP
BLOCKS = 3
BLOCK = SLOTS // BLOCKS
PIECES = D // 128
WIDE = SLOTS * PIECES
SCALE = HS ** (-0.5)
BF = jnp.bfloat16
F32 = jnp.float32
MIB = 1024 * 1024


def mm(a, b):
    return jnp.dot(a, b, preferred_element_type=F32)


def mm_nt(a, b):
    return lax.dot_general(a, b, (((1,), (1,)), ((), ())), preferred_element_type=F32)


def mm_tn(a, b):
    return lax.dot_general(a, b, (((0,), (0,)), ((), ())), preferred_element_type=F32)


def iota(shape, dim):
    return lax.broadcasted_iota(jnp.int32, shape, dim)


def chosen_by_row(ids):
    lanes = iota((ROWS, EXPERTS), 1)
    hit = ids[:, 0:1] == lanes
    for k in range(1, TOPK):
        hit = hit | (ids[:, k : k + 1] == lanes)
    return hit


def chosen_by_expert(ids_t):
    subs = iota((EXPERTS, ROWS), 0)
    hit = ids_t[0:1, :] == subs
    for k in range(1, TOPK):
        hit = hit | (ids_t[k : k + 1, :] == subs)
    return hit


def to_bf(mask):
    return jnp.where(mask, 1.0, 0.0).astype(BF)


def expert_of(slot):
    return (slot * 43691) >> 18


def spread_by_slot():
    return to_bf(expert_of(iota((SLOTS, EXPERTS), 0)) == iota((SLOTS, EXPERTS), 1))


def spread_by_expert():
    return to_bf(expert_of(iota((EXPERTS, SLOTS), 1)) == iota((EXPERTS, SLOTS), 0))


def slots_by_expert(ids_t):
    hit = chosen_by_expert(ids_t)
    before = to_bf(iota((ROWS, ROWS), 0) < iota((ROWS, ROWS), 1))
    return jnp.where(hit, mm(to_bf(hit), before), -1.0)


def dispatch_matrix(ids_t):
    slot = mm(spread_by_slot(), slots_by_expert(ids_t).astype(BF)).astype(jnp.int32)
    at = iota((SLOTS, ROWS), 0)
    return to_bf(slot == at - expert_of(at) * CAP)


def combine_matrix(ids):
    hit = chosen_by_row(ids)
    before = to_bf(iota((ROWS, ROWS), 1) < iota((ROWS, ROWS), 0))
    slot = jnp.where(hit, mm(before, to_bf(hit)), -1.0).astype(BF)
    slot = mm(slot, spread_by_expert()).astype(jnp.int32)
    at = iota((ROWS, SLOTS), 1)
    return slot == at - expert_of(at) * CAP


def to_wide(value, first, wide):
    for c in range(value.shape[1] // 128):
        wide[pl.ds(first + c, SLOTS, stride=PIECES), :] = value[:, c * 128 : (c + 1) * 128]


def copy_rows(src, dst):
    step = WIDE // 16

    @pl.loop(0, 16)
    def _(i):
        rows = pl.ds(pl.multiple_of(i * step, step), step)
        dst[rows, :] = src[rows, :].astype(dst.dtype)


def row_copies(src, dst, sems):
    step = BLOCK * PIECES
    return [
        pltpu.make_async_copy(src.at[pl.ds(m * step, step)], dst.at[pl.ds(m * step, step)], sems.at[m])
        for m in range(BLOCKS)
    ]


def from_wide(copies, stage, wide, dst, scale=None):
    step = BLOCK * PIECES
    for m in range(BLOCKS):
        copies[m].wait()

        @pl.loop(0, 4)
        def _(i):
            rows = pl.ds(pl.multiple_of(m * step + i * (step // 4), step // 4), step // 4)
            wide[rows, :] = stage[rows, :].astype(F32)

        at = slice(m * BLOCK, (m + 1) * BLOCK)
        for c in range(PIECES):
            part = wide[pl.ds(m * step + c, BLOCK, stride=PIECES), :]
            if scale is not None:
                part = part * scale[at]
            dst[at, c * 128 : (c + 1) * 128] = part.astype(BF)


def send_rows(product, stage, wide, copies):
    step = BLOCK * PIECES
    for m in range(BLOCKS):
        rows = slice(m * BLOCK, (m + 1) * BLOCK)
        for n in range(8):
            value = product(rows, n)
            for c in range(2):
                wide[pl.ds(m * step + 2 * n + c, BLOCK, stride=PIECES), :] = value[:, c * 128 : (c + 1) * 128]

        @pl.loop(0, 4)
        def _(i):
            part = pl.ds(pl.multiple_of(m * step + i * (step // 4), step // 4), step // 4)
            stage[part, :] = wide[part, :].astype(BF)

        copies[m].start()


def split(value):
    high = value.astype(BF)
    return high, (value - high.astype(F32)).astype(BF)


def grad_pack_kernel(ids_t_ref, live_ref, grad_ref, out_ref, wide):
    select = dispatch_matrix(ids_t_ref[...])
    grad = jnp.where(live_ref[...] > 0, grad_ref[...].astype(F32), 0.0).astype(BF)
    for n in range(8):
        to_wide(mm(select, grad[:, n * 256 : (n + 1) * 256]), 2 * n, wide)
    copy_rows(wide, out_ref)


def allowed_own():
    key = iota((ROWS, ROWS), 0)
    row = iota((ROWS, ROWS), 1)
    return ((key >> 6) == (row >> 6)) & ((key & 63) <= (row & 63))


def attention_kernel(q_ref, rk_ref, rv_ref, prefix_ref, out_ref, lse_ref):
    mask = allowed_own()
    for kv in range(KV):
        lanes = slice(kv * HS, (kv + 1) * HS)
        vlanes = slice((KV + kv) * HS, (KV + kv + 1) * HS)
        keys = jnp.concatenate([prefix_ref[:, lanes], rk_ref[:, lanes]], axis=0)
        values = jnp.concatenate([prefix_ref[:, vlanes], rv_ref[:, lanes]], axis=0)
        values_t = values.astype(F32).T.astype(BF)
        for g in range(GROUP):
            h = kv * GROUP + g
            cols = slice(h * HS, (h + 1) * HS)
            scores = mm_nt(keys, q_ref[:, cols]) * SCALE
            near = jnp.where(mask, scores[PREFIX:], -1e30)
            scores = jnp.concatenate([scores[:PREFIX], near], axis=0)
            top = jnp.max(scores, axis=0, keepdims=True)
            probs = jnp.exp(scores - top)
            total = jnp.sum(probs, axis=0, keepdims=True)
            low = (probs * (1.0 / total)).astype(BF)
            out_ref[:, cols] = mm(values_t, low).T.astype(BF)
            lse_ref[h : h + 1, :] = top + jnp.log(total)


def project_own_kernel(core_ref, attn_ref, w_ref, resid_ref, xmid_ref):
    part = mm(attn_ref[...], w_ref[...])

    @pl.when(pl.program_id(0) == 0)
    def _():
        xmid_ref[...] = resid_ref[...].astype(F32) + part

    @pl.when(pl.program_id(0) > 0)
    def _():
        xmid_ref[...] += part


def project_kernel(
    core_ref, attn_ref, w_ref, part_ref, gain_ref, router_ref, ids_ref, ids_t_ref,
    xmid_ref, hidden_ref, gates_ref, slot_gates_ref, out_ref, wide,
):
    step = pl.program_id(0)
    part = mm(attn_ref[...], w_ref[...])

    @pl.when(step == 0)
    def _():
        xmid_ref[...] = part_ref[...] + part

    @pl.when(step > 0)
    def _():
        xmid_ref[...] += part

    @pl.when(step == pl.num_programs(0) - 1)
    def _():
        xmid = xmid_ref[...]
        rinv = lax.rsqrt(jnp.mean(xmid * xmid, axis=-1, keepdims=True) + 1e-06)
        hidden = (xmid * rinv * gain_ref[...]).astype(BF)
        hidden_ref[...] = hidden
        select = dispatch_matrix(ids_t_ref[...])
        for n in range(8):
            to_wide(mm(select, hidden[:, n * 256 : (n + 1) * 256]), 2 * n, wide)
        copy_rows(wide, out_ref)
        logits = mm(hidden, router_ref[...])
        chosen = jnp.where(chosen_by_row(ids_ref[...]), jnp.exp(logits), 0.0)
        gates = chosen / jnp.sum(chosen, axis=1, keepdims=True)
        gates_ref[...] = gates
        gates_t = gates.T
        slot = slots_by_expert(ids_t_ref[...]).astype(jnp.int32)
        lane = iota((EXPERTS, 128), 1)
        slot_gates = jnp.zeros((EXPERTS, 128), F32)
        for i in range(CAP):
            column = jnp.sum(jnp.where(slot == i, gates_t, 0.0), axis=1, keepdims=True)
            slot_gates = slot_gates + jnp.where(lane == i, column, 0.0)
        slot_gates_ref[...] = slot_gates


def expert_kernel(
    x_hbm, wg_hbm, wu_hbm, wd_hbm, out_hbm, xc_hbm, act_hbm, pg_hbm, pu_hbm,
    wg, wu, wd, xc, act, pg, pu, wide, stage, row_sem, in_sem, out_sem, send_sem,
):
    arrivals = row_copies(x_hbm, stage, row_sem)
    for arrival in arrivals:
        arrival.start()
    loads = [
        pltpu.make_async_copy(src, dst, in_sem.at[i])
        for i, (src, dst) in enumerate(((wg_hbm, wg), (wu_hbm, wu), (wd_hbm, wd)))
    ]
    for load in loads:
        load.start()
    stores = [
        pltpu.make_async_copy(src, dst, out_sem.at[i])
        for i, (src, dst) in enumerate(((xc, xc_hbm), (act, act_hbm), (pg, pg_hbm), (pu, pu_hbm)))
    ]
    from_wide(arrivals, stage, wide, xc)
    stores[0].start()
    loads[0].wait()
    loads[1].wait()

    @pl.loop(0, 3)
    def _(n):
        cols = pl.ds(pl.multiple_of(n * 256, 256), 256)
        gate = mm(xc[...], wg[:, cols])
        up = mm(xc[...], wu[:, cols])
        pg[:, cols] = gate
        pu[:, cols] = up
        act[:, cols] = (gate * jax.nn.sigmoid(gate) * up).astype(BF)

    loads[2].wait()
    departures = row_copies(stage, out_hbm, send_sem)
    send_rows(lambda rows, n: mm(act[rows, :], wd[:, n * 256 : (n + 1) * 256]), stage, wide, departures)
    for store in stores[1:]:
        store.start()
    for store in departures + stores:
        store.wait()


def expert_back_kernel(
    slot_gates_ref, g_hbm, pg_hbm, pu_hbm, wd_hbm, wg_hbm, wu_hbm, back_hbm, ob_hbm, pb_hbm, ub_hbm,
    wd, wg, wu, ob, pb, ub, pg, pu, wide, stage, row_sem, in_sem, out_sem, send_sem,
):
    arrivals = row_copies(g_hbm, stage, row_sem)
    for arrival in arrivals:
        arrival.start()
    loads = [
        pltpu.make_async_copy(src, dst, in_sem.at[i])
        for i, (src, dst) in enumerate(((wd_hbm, wd), (pg_hbm, pg), (pu_hbm, pu), (wg_hbm, wg), (wu_hbm, wu)))
    ]
    for load in loads:
        load.start()
    stores = [
        pltpu.make_async_copy(src, dst, out_sem.at[i])
        for i, (src, dst) in enumerate(((ob, ob_hbm), (pb, pb_hbm), (ub, ub_hbm)))
    ]
    high, low = split(slot_gates_ref[...])
    spread = spread_by_slot()
    gates = mm(spread, high) + mm(spread, low)
    at = iota((SLOTS, 128), 0)
    mine = iota((SLOTS, 128), 1) == at - expert_of(at) * CAP
    gates = jnp.sum(jnp.where(mine, gates, 0.0), axis=1, keepdims=True)
    from_wide(arrivals, stage, wide, ob, gates)
    stores[0].start()
    for load in loads[:3]:
        load.wait()

    @pl.loop(0, 3)
    def _(n):
        cols = pl.ds(pl.multiple_of(n * 256, 256), 256)
        act_back = mm_nt(ob[...], wd[cols, :])
        gate = pg[:, cols]
        sig = jax.nn.sigmoid(gate)
        pb[:, cols] = (act_back * pu[:, cols] * (sig * (1.0 + gate * (1.0 - sig)))).astype(BF)
        ub[:, cols] = (act_back * (gate * sig)).astype(BF)

    stores[1].start()
    stores[2].start()
    loads[3].wait()
    loads[4].wait()

    def product(rows, n):
        cols = slice(n * 256, (n + 1) * 256)
        return mm_nt(pb[rows, :], wg[cols, :]) + mm_nt(ub[rows, :], wu[cols, :])

    departures = row_copies(stage, back_hbm, send_sem)
    send_rows(product, stage, wide, departures)
    for store in departures + stores:
        store.wait()


def weight_grad_kernel(xc_ref, ob_ref, act_ref, pb_ref, ub_ref, gate_ref, up_ref, down_ref, act_t):
    @pl.when(pl.program_id(0) == 0)
    def _():
        act_t[...] = act_ref[...].astype(F32).T.astype(BF)

    xt = xc_ref[...].astype(F32).T.astype(BF)
    gate_ref[...] = mm(xt, pb_ref[...]).astype(BF)
    up_ref[...] = mm(xt, ub_ref[...]).astype(BF)
    down_ref[...] = mm(act_t[...], ob_ref[...]).astype(BF)


def owner_kernel(
    rows_hbm, xmid_ref, hidden_ref, gates_ref, grad_ref, live_ref, ids_ref, layer_ref, logit_back_ref, sums_ref,
    wide, stage, rows, row_sem,
):
    arrivals = row_copies(rows_hbm, stage, row_sem)
    for arrival in arrivals:
        arrival.start()
    from_wide(arrivals, stage, wide, rows)
    select = combine_matrix(ids_ref[...])
    grad = jnp.where(live_ref[...] > 0, grad_ref[...].astype(F32), 0.0).astype(BF)
    product = jnp.where(select, mm_nt(grad, rows[...]), 0.0)
    spread = spread_by_slot()
    high, low = split(product)
    gate_back = mm(high, spread) + mm(low, spread)
    gates = gates_ref[...]
    route = gates * (gate_back - jnp.sum(gates * gate_back, axis=1, keepdims=True))
    logit_back = route.astype(BF)
    logit_back_ref[...] = logit_back
    sums_ref[...] = mm_tn(hidden_ref[...], logit_back).astype(BF)
    high, low = split(gates)
    spread = spread_by_expert()
    weight = jnp.where(select, mm(high, spread) + mm(low, spread), 0.0)
    high, low = split(weight)
    for j in range(4):
        cols = slice(j * 512, (j + 1) * 512)
        part = rows[:, cols]
        layer_ref[:, cols] = (xmid_ref[:, cols] + (mm(high, part) + mm(low, part))).astype(BF)


def back_kernel(
    core_ref, rows_hbm, xmid_ref, logit_back_ref, grad_ref, live_ref, ids_ref, gain_ref, router_ref, w_ref, w_other_ref,
    resid_ref, gain_sum_ref, attn_back_ref, acc, wide, stage, rows, row_sem,
):
    @pl.when(pl.program_id(0) == 0)
    def _():
        arrivals = row_copies(rows_hbm, stage, row_sem)
        for arrival in arrivals:
            arrival.start()
        from_wide(arrivals, stage, wide, rows)
        select = to_bf(combine_matrix(ids_ref[...]))
        xmid = xmid_ref[...]
        rinv = lax.rsqrt(jnp.mean(xmid * xmid, axis=-1, keepdims=True) + 1e-06)
        mean = jnp.zeros((ROWS, 1), F32)
        for j in range(4):
            cols = slice(j * 512, (j + 1) * 512)
            value = mm(select, rows[:, cols]) + mm_nt(logit_back_ref[...], router_ref[cols, :])
            normed = xmid[:, cols] * rinv
            partial = jnp.sum(value * normed, axis=0, keepdims=True)
            for c in range(4):
                gain_sum_ref[4 * j + c : 4 * j + c + 1, :] = partial[:, c * 128 : (c + 1) * 128]
            value = value * gain_ref[:, cols]
            acc[:, cols] = value
            mean = mean + jnp.sum(value * normed, axis=-1, keepdims=True)
        mean = mean * (1.0 / D)
        grad = jnp.where(live_ref[...] > 0, grad_ref[...].astype(F32), 0.0)
        resid_ref[...] = (grad + rinv * (acc[...] - xmid * rinv * mean)).astype(BF)

    first = core_ref[0] == 0
    near, far = w_ref[...], w_other_ref[...]
    half = near.shape[0]
    value = mm_nt(resid_ref[...], jnp.concatenate([near, far], axis=0)).astype(BF)

    @pl.when(first)
    def _():
        attn_back_ref[...] = value

    @pl.when(jnp.logical_not(first))
    def _():
        attn_back_ref[:, 0:half] = value[:, half:]
        attn_back_ref[:, half:] = value[:, 0:half]


def attention_back_kernel(q_ref, rk_ref, rv_ref, prefix_ref, lse_ref, ab_ref, dq_ref, dk_ref, dv_ref, *rest):
    dprefix, (ds_all, p_all) = rest[:N_RESP], rest[N_RESP:]
    mask = allowed_own()
    for kv in range(KV):
        lanes = slice(kv * HS, (kv + 1) * HS)
        vlanes = slice((KV + kv) * HS, (KV + kv + 1) * HS)
        keys = jnp.concatenate([prefix_ref[:, lanes], rk_ref[:, lanes]], axis=0)
        values = jnp.concatenate([prefix_ref[:, vlanes], rv_ref[:, lanes]], axis=0)
        keys_t = keys.astype(F32).T.astype(BF)
        q_parts = []
        ab_parts = []
        for g in range(GROUP):
            h = kv * GROUP + g
            cols = slice(h * HS, (h + 1) * HS)
            q = q_ref[:, cols]
            ab = ab_ref[:, cols]
            q_parts.append(q)
            ab_parts.append(ab)
            scores = mm_nt(keys, q) * SCALE
            near = jnp.where(mask, scores[PREFIX:], -1e30)
            scores = jnp.concatenate([scores[:PREFIX], near], axis=0)
            probs = jnp.exp(scores - lse_ref[h : h + 1, :])
            prob_back = mm_nt(values, ab)
            delta = jnp.sum(probs * prob_back, axis=0, keepdims=True)
            score_back = (probs * (prob_back - delta) * SCALE).astype(BF)
            at = slice(g * ROWS, (g + 1) * ROWS)
            p_all[:, at] = probs.astype(BF)
            ds_all[:, at] = score_back
            dq_ref[:, cols] = mm(keys_t, score_back).T.astype(BF)
        dk = mm(ds_all[...], jnp.concatenate(q_parts, axis=0)).astype(BF)
        dv = mm(p_all[...], jnp.concatenate(ab_parts, axis=0)).astype(BF)
        for r in range(N_RESP):
            at = slice(r * SHARE, (r + 1) * SHARE)
            dprefix[r][:, lanes] = dk[at]
            dprefix[r][:, vlanes] = dv[at]
        dk_ref[:, lanes] = dk[PREFIX:]
        dv_ref[:, lanes] = dv[PREFIX:]


def struct(shape, dtype):
    return jax.ShapeDtypeStruct(shape, dtype)


def params(limit):
    return pltpu.CompilerParams(vmem_limit_bytes=limit * MIB)


def cost(flops, moved):
    return pl.CostEstimate(flops=int(flops), bytes_accessed=int(moved), transcendentals=0)


VMEM_SPEC = pl.BlockSpec(memory_space=pltpu.VMEM)
ANY_SPEC = pl.BlockSpec(memory_space=pl.ANY)


def whole(shape):
    return pl.BlockSpec(shape, lambda *at: (0,) * len(shape))


def swap(value, mask):
    return lax.ppermute(value, "resp", [(i, i ^ mask) for i in range(N_RESP)])


def exchange(block):
    moved = lax.all_to_all(
        block.reshape(DEVICES, CAP * PIECES, 128), ("prompt", "resp"), split_axis=0, concat_axis=0, tiled=True
    )
    return moved.reshape(WIDE, 128)


def shards(
    queries, response_keys, response_values, prefix_keys, prompt_values, resid, out_proj, router, norm_gain,
    w_gate, w_up, w_down, expert_ids, lengths, out_grad,
):
    r_at = lax.axis_index("resp")
    ids = expert_ids.reshape(ROWS, TOPK)
    ids_t = ids.T
    live = (jnp.arange(SPAN, dtype=jnp.int32)[None, :] < lengths[0][:, None]).astype(F32).reshape(ROWS, 1)
    grad = out_grad.reshape(ROWS, D)
    q = queries.reshape(ROWS, D)
    rk = response_keys.reshape(ROWS, KV * HS)
    rv = response_values.reshape(ROWS, KV * HS)
    gain = norm_gain.reshape(1, D)

    half = D // N_PROMPT // 2
    core = r_at % 2
    w_own = lax.dynamic_slice(out_proj, (core * half, 0), (half, D))
    w_own = lax.all_gather(w_own, "prompt", axis=0, tiled=True)
    core = core.astype(jnp.int32).reshape(1)

    prefix_part = jnp.concatenate([prefix_keys[0], prompt_values[0]], axis=1)
    prefix = jnp.concatenate([prefix_part] + [swap(prefix_part, i) for i in range(1, N_RESP)], axis=0)

    grad_rows = pl.pallas_call(
        grad_pack_kernel,
        out_shape=struct((WIDE, 128), BF),
        in_specs=[VMEM_SPEC] * 3,
        out_specs=VMEM_SPEC,
        scratch_shapes=[pltpu.VMEM((WIDE, 128), F32)],
        compiler_params=params(32),
        cost_estimate=cost(1.2e9, 4e6),
        name="grad_pack",
    )(ids_t, live, grad)
    grad_rows = exchange(grad_rows)

    attn, lse = pl.pallas_call(
        attention_kernel,
        out_shape=(struct((ROWS, D), BF), struct((HEADS, ROWS), F32)),
        in_specs=[VMEM_SPEC] * 4,
        out_specs=(VMEM_SPEC, VMEM_SPEC),
        compiler_params=params(32),
        cost_estimate=cost(4e9, 2e6),
        name="attention",
    )(q, rk, rv, prefix)
    w_own, attn, grad_rows = lax.optimization_barrier((w_own, attn, grad_rows))
    w_other = swap(w_own, 1)

    steps = N_PROMPT
    w_spec = pl.BlockSpec((half, D), lambda i, c: (i, 0))
    xmid = pl.pallas_call(
        project_own_kernel,
        grid_spec=pltpu.PrefetchScalarGridSpec(
            num_scalar_prefetch=1,
            grid=(steps,),
            in_specs=[pl.BlockSpec((ROWS, half), lambda i, c: (0, 2 * i + c[0])), w_spec, whole((ROWS, D))],
            out_specs=whole((ROWS, D)),
        ),
        out_shape=struct((ROWS, D), F32),
        compiler_params=params(32),
        cost_estimate=cost(0.6e9, 6e6),
        name="project_own",
    )(core, attn, w_own, resid.reshape(ROWS, D))
    xmid, hidden, gates, slot_gates, x_rows = pl.pallas_call(
        project_kernel,
        grid_spec=pltpu.PrefetchScalarGridSpec(
            num_scalar_prefetch=1,
            grid=(steps,),
            in_specs=[
                pl.BlockSpec((ROWS, half), lambda i, c: (0, 2 * i + 1 - c[0])), w_spec, whole((ROWS, D)), whole((1, D)), whole((D, EXPERTS)), whole((ROWS, TOPK)), whole((TOPK, ROWS)),
            ],
            out_specs=(
                whole((ROWS, D)), whole((ROWS, D)), whole((ROWS, EXPERTS)), whole((EXPERTS, 128)), whole((WIDE, 128))
            ),
            scratch_shapes=[pltpu.VMEM((WIDE, 128), F32)],
        ),
        out_shape=(
            struct((ROWS, D), F32), struct((ROWS, D), BF), struct((ROWS, EXPERTS), F32), struct((EXPERTS, 128), F32),
            struct((WIDE, 128), BF),
        ),
        compiler_params=params(40),
        cost_estimate=cost(3e9, 14e6),
        name="project",
    )(core, attn, w_other, xmid, gain, router, ids, ids_t)
    x_rows = exchange(x_rows)
    x_rows, slot_gates = lax.optimization_barrier((x_rows, slot_gates))
    slot_gates = lax.all_to_all(
        slot_gates.reshape(DEVICES, 1, 128), ("prompt", "resp"), split_axis=0, concat_axis=0, tiled=True
    ).reshape(DEVICES, 128)

    weights = [pltpu.VMEM((D, FF), BF), pltpu.VMEM((D, FF), BF), pltpu.VMEM((FF, D), BF)]
    wide = [pltpu.VMEM((WIDE, 128), F32), pltpu.VMEM((WIDE, 128), BF)]
    out_rows, xc, act, pg, pu = pl.pallas_call(
        expert_kernel,
        out_shape=(
            struct((WIDE, 128), BF), struct((SLOTS, D), BF), struct((SLOTS, FF), BF), struct((SLOTS, FF), F32),
            struct((SLOTS, FF), F32),
        ),
        in_specs=[ANY_SPEC] * 4,
        out_specs=(ANY_SPEC,) * 5,
        scratch_shapes=weights
        + [
            pltpu.VMEM((SLOTS, D), BF), pltpu.VMEM((SLOTS, FF), BF), pltpu.VMEM((SLOTS, FF), F32),
            pltpu.VMEM((SLOTS, FF), F32),
        ]
        + wide
        + [pltpu.SemaphoreType.DMA((n,)) for n in (BLOCKS, 3, 4, BLOCKS)],
        compiler_params=params(48),
        cost_estimate=cost(8e9, 26e6),
        name="expert",
    )(x_rows, w_gate[0], w_up[0], w_down[0])
    out_rows = exchange(out_rows)

    back_rows, ob, pb, ub = pl.pallas_call(
        expert_back_kernel,
        out_shape=(
            struct((WIDE, 128), BF), struct((SLOTS, D), BF), struct((SLOTS, FF), BF), struct((SLOTS, FF), BF)
        ),
        in_specs=[VMEM_SPEC] + [ANY_SPEC] * 6,
        out_specs=(ANY_SPEC,) * 4,
        scratch_shapes=[weights[2], weights[0], weights[1]]
        + [
            pltpu.VMEM((SLOTS, D), BF), pltpu.VMEM((SLOTS, FF), BF), pltpu.VMEM((SLOTS, FF), BF),
            pltpu.VMEM((SLOTS, FF), F32), pltpu.VMEM((SLOTS, FF), F32),
        ]
        + wide
        + [pltpu.SemaphoreType.DMA((n,)) for n in (BLOCKS, 5, 3, BLOCKS)],
        compiler_params=params(48),
        cost_estimate=cost(8e9, 26e6),
        name="expert_back",
    )(slot_gates, grad_rows, pg, pu, w_down[0], w_gate[0], w_up[0])
    back_rows = exchange(back_rows)

    layer_out, logit_back, sums = pl.pallas_call(
        owner_kernel,
        out_shape=(struct((ROWS, D), BF), struct((ROWS, EXPERTS), BF), struct((D, EXPERTS), BF)),
        in_specs=[ANY_SPEC] + [VMEM_SPEC] * 6,
        out_specs=(VMEM_SPEC,) * 3,
        scratch_shapes=wide + [pltpu.VMEM((SLOTS, D), BF), pltpu.SemaphoreType.DMA((BLOCKS,))],
        compiler_params=params(40),
        cost_estimate=cost(3e9, 9e6),
        name="owner",
    )(out_rows, xmid, hidden, gates, grad, live, ids)

    weight_grads = pl.pallas_call(
        weight_grad_kernel,
        grid=(8,),
        out_shape=(struct((D, FF), BF), struct((D, FF), BF), struct((FF, D), BF)),
        in_specs=[
            pl.BlockSpec((SLOTS, 256), lambda i: (0, i)), pl.BlockSpec((SLOTS, 256), lambda i: (0, i)),
            whole((SLOTS, FF)), whole((SLOTS, FF)), whole((SLOTS, FF)),
        ],
        out_specs=(
            pl.BlockSpec((256, FF), lambda i: (i, 0)), pl.BlockSpec((256, FF), lambda i: (i, 0)),
            pl.BlockSpec((FF, 256), lambda i: (0, i)),
        ),
        scratch_shapes=[pltpu.VMEM((FF, SLOTS), BF)],
        compiler_params=params(32),
        cost_estimate=cost(7.3e9, 20e6),
        name="weight_grad",
    )(xc, ob, act, pb, ub)
    back_rows, sums, weight_grads = lax.optimization_barrier((back_rows, sums, weight_grads))
    gate_grad, up_grad, down_grad = weight_grads

    piece = D // DEVICES
    sums = lax.all_to_all(
        sums.reshape(DEVICES, piece, EXPERTS), ("prompt", "resp"), split_axis=0, concat_axis=0, tiled=True
    )

    resid_grad, gain_sum, attn_back = pl.pallas_call(
        back_kernel,
        grid_spec=pltpu.PrefetchScalarGridSpec(
            num_scalar_prefetch=1,
            grid=(steps,),
            in_specs=[
                ANY_SPEC, whole((ROWS, D)), whole((ROWS, EXPERTS)), whole((ROWS, D)), whole((ROWS, 1)),
                whole((ROWS, TOPK)), whole((1, D)), whole((D, EXPERTS)), w_spec, w_spec,
            ],
            out_specs=(whole((ROWS, D)), whole((PIECES, 128)), pl.BlockSpec((ROWS, 2 * half), lambda i, c: (0, i))),
            scratch_shapes=[pltpu.VMEM((ROWS, D), F32)]
            + wide
            + [pltpu.VMEM((SLOTS, D), BF), pltpu.SemaphoreType.DMA((BLOCKS,))],
        ),
        out_shape=(struct((ROWS, D), BF), struct((PIECES, 128), F32), struct((ROWS, D), BF)),
        compiler_params=params(48),
        cost_estimate=cost(3e9, 16e6),
        name="back",
    )(core, back_rows, xmid, logit_back, grad, live, ids, gain, router, w_own, w_other)

    sums = jnp.sum(sums.astype(F32), axis=0)
    sums = jnp.concatenate([sums, gain_sum], axis=0).astype(BF)
    sums = lax.all_to_all(
        jnp.broadcast_to(sums[None], (DEVICES, piece + PIECES, EXPERTS)),
        ("prompt", "resp"), split_axis=0, concat_axis=0, tiled=True,
    ).astype(F32)
    router_grad = sums[:, :piece].reshape(D, EXPERTS)
    gain_grad = jnp.sum(sums[:, piece:], axis=0).reshape(D)

    query_grad, resp_key_grad, resp_value_grad, *prefix_parts = pl.pallas_call(
        attention_back_kernel,
        out_shape=(
            struct((ROWS, D), BF), struct((ROWS, KV * HS), BF), struct((ROWS, KV * HS), BF),
        )
        + (struct((SHARE, 2 * KV * HS), BF),) * N_RESP,
        in_specs=[VMEM_SPEC] * 6,
        out_specs=(VMEM_SPEC,) * (3 + N_RESP),
        scratch_shapes=[pltpu.VMEM((PREFIX + ROWS, GROUP * ROWS), BF)] * 2,
        compiler_params=params(32),
        cost_estimate=cost(8e9, 4e6),
        name="attention_back",
    )(q, rk, rv, prefix, lse, attn_back)

    prefix_grad = prefix_parts[0].astype(F32)
    for i in range(1, N_RESP):
        prefix_grad = prefix_grad + swap(prefix_parts[i], i).astype(F32)
    prefix_grad = prefix_grad.astype(BF)

    rows_shape = (1, ROWS // SPAN, SPAN, D)
    near_shape = (1, ROWS // SPAN, SPAN, KV * HS)
    return (
        layer_out.reshape(rows_shape),
        resid_grad.reshape(rows_shape),
        query_grad.reshape(rows_shape),
        resp_key_grad.reshape(near_shape),
        resp_value_grad.reshape(near_shape),
        prefix_grad[None, :, : KV * HS],
        prefix_grad[None, :, KV * HS :],
        router_grad,
        gain_grad,
        gate_grad[None],
        up_grad[None],
        down_grad[None],
    )


def solution(mesh):
    in_specs = (
        P("prompt", "resp", None, None),
        P("prompt", "resp", None, None),
        P("prompt", "resp", None, None),
        P("prompt", "resp", None),
        P("prompt", "resp", None),
        P("prompt", "resp", None, None),
        P("prompt", None),
        P(),
        P(),
        P(("prompt", "resp"), None, None),
        P(("prompt", "resp"), None, None),
        P(("prompt", "resp"), None, None),
        P("prompt", "resp", None, None),
        P("prompt", "resp"),
        P("prompt", "resp", None, None),
    )
    out_specs = (
        P("prompt", "resp", None, None),
        P("prompt", "resp", None, None),
        P("prompt", "resp", None, None),
        P("prompt", "resp", None, None),
        P("prompt", "resp", None, None),
        P("prompt", "resp", None),
        P("prompt", "resp", None),
        P(),
        P(),
        P(("prompt", "resp"), None, None),
        P(("prompt", "resp"), None, None),
        P(("prompt", "resp"), None, None),
    )
    return jax.shard_map(shards, mesh=mesh, in_specs=in_specs, out_specs=out_specs, check_vma=False)
```

```python
import jax
import jax.numpy as jnp
from jax import lax
from jax.experimental import pallas as pl
from jax.experimental.pallas import tpu as pltpu
from jax.sharding import PartitionSpec as P

D = 2048
HEADS = 16
KV = 2
GROUP = HEADS // KV
HS = 128
FF = 768
TOPK = 4
PREFIX = 512
SPAN = 64
ROWS = 128
EXPERTS = 128
CAP = 6
N_PROMPT = 8
N_RESP = 16
DEVICES = 128
SLOTS = DEVICES * CAP
SHARE = PREFIX // N_RESP
BLOCKS = 3
BLOCK = SLOTS // BLOCKS
PIECES = D // 128
WIDE = SLOTS * PIECES
SCALE = HS ** (-0.5)
BF = jnp.bfloat16
F32 = jnp.float32
MIB = 1024 * 1024


def mm(a, b):
    return jnp.dot(a, b, preferred_element_type=F32)


def mm_nt(a, b):
    return lax.dot_general(a, b, (((1,), (1,)), ((), ())), preferred_element_type=F32)


def mm_tn(a, b):
    return lax.dot_general(a, b, (((0,), (0,)), ((), ())), preferred_element_type=F32)


def iota(shape, dim):
    return lax.broadcasted_iota(jnp.int32, shape, dim)


def chosen_by_row(ids):
    lanes = iota((ROWS, EXPERTS), 1)
    hit = ids[:, 0:1] == lanes
    for k in range(1, TOPK):
        hit = hit | (ids[:, k : k + 1] == lanes)
    return hit


def chosen_by_expert(ids_t):
    subs = iota((EXPERTS, ROWS), 0)
    hit = ids_t[0:1, :] == subs
    for k in range(1, TOPK):
        hit = hit | (ids_t[k : k + 1, :] == subs)
    return hit


def to_bf(mask):
    return jnp.where(mask, 1.0, 0.0).astype(BF)


def expert_of(slot):
    return (slot * 43691) >> 18


def spread_by_slot():
    return to_bf(expert_of(iota((SLOTS, EXPERTS), 0)) == iota((SLOTS, EXPERTS), 1))


def spread_by_expert():
    return to_bf(expert_of(iota((EXPERTS, SLOTS), 1)) == iota((EXPERTS, SLOTS), 0))


def slots_by_expert(ids_t):
    hit = chosen_by_expert(ids_t)
    before = to_bf(iota((ROWS, ROWS), 0) < iota((ROWS, ROWS), 1))
    return jnp.where(hit, mm(to_bf(hit), before), -1.0)


def dispatch_matrix(ids_t):
    slot = mm(spread_by_slot(), slots_by_expert(ids_t).astype(BF)).astype(jnp.int32)
    at = iota((SLOTS, ROWS), 0)
    return to_bf(slot == at - expert_of(at) * CAP)


def combine_matrix(ids):
    hit = chosen_by_row(ids)
    before = to_bf(iota((ROWS, ROWS), 1) < iota((ROWS, ROWS), 0))
    slot = jnp.where(hit, mm(before, to_bf(hit)), -1.0).astype(BF)
    slot = mm(slot, spread_by_expert()).astype(jnp.int32)
    at = iota((ROWS, SLOTS), 1)
    return slot == at - expert_of(at) * CAP


def to_wide(value, first, wide):
    for c in range(value.shape[1] // 128):
        wide[pl.ds(first + c, SLOTS, stride=PIECES), :] = value[:, c * 128 : (c + 1) * 128]


def copy_rows(src, dst):
    step = WIDE // 16

    @pl.loop(0, 16)
    def _(i):
        rows = pl.ds(pl.multiple_of(i * step, step), step)
        dst[rows, :] = src[rows, :].astype(dst.dtype)


def row_copies(src, dst, sems):
    step = BLOCK * PIECES
    return [
        pltpu.make_async_copy(src.at[pl.ds(m * step, step)], dst.at[pl.ds(m * step, step)], sems.at[m])
        for m in range(BLOCKS)
    ]


def from_wide(copies, stage, wide, dst):
    step = BLOCK * PIECES
    for m in range(BLOCKS):
        copies[m].wait()

        @pl.loop(0, 4)
        def _(i):
            rows = pl.ds(pl.multiple_of(m * step + i * (step // 4), step // 4), step // 4)
            wide[rows, :] = stage[rows, :].astype(F32)

        at = slice(m * BLOCK, (m + 1) * BLOCK)
        for c in range(PIECES):
            part = wide[pl.ds(m * step + c, BLOCK, stride=PIECES), :]
            dst[at, c * 128 : (c + 1) * 128] = part.astype(BF)


def send_rows(product, stage, wide, copies):
    step = BLOCK * PIECES
    for m in range(BLOCKS):
        rows = slice(m * BLOCK, (m + 1) * BLOCK)
        for n in range(8):
            value = product(rows, n)
            for c in range(2):
                wide[pl.ds(m * step + 2 * n + c, BLOCK, stride=PIECES), :] = value[:, c * 128 : (c + 1) * 128]

        @pl.loop(0, 4)
        def _(i):
            part = pl.ds(pl.multiple_of(m * step + i * (step // 4), step // 4), step // 4)
            stage[part, :] = wide[part, :].astype(BF)

        copies[m].start()


def split(value):
    high = value.astype(BF)
    return high, (value - high.astype(F32)).astype(BF)


def grad_pack_kernel(ids_t_ref, live_ref, grad_ref, gates_ref, out_ref, wide):
    select = dispatch_matrix(ids_t_ref[...])
    high, low = split(gates_ref[...])
    mine = expert_of(iota((SLOTS, EXPERTS), 0)) == iota((SLOTS, EXPERTS), 1)
    scale = jnp.sum(jnp.where(mine, mm(select, high) + mm(select, low), 0.0), axis=1, keepdims=True)
    grad = jnp.where(live_ref[...] > 0, grad_ref[...].astype(F32), 0.0).astype(BF)
    for n in range(8):
        to_wide(scale * mm(select, grad[:, n * 256 : (n + 1) * 256]), 2 * n, wide)
    copy_rows(wide, out_ref)


def allowed_own():
    key = iota((ROWS, ROWS), 0)
    row = iota((ROWS, ROWS), 1)
    return ((key >> 6) == (row >> 6)) & ((key & 63) <= (row & 63))


def attention_kernel(q_ref, rk_ref, rv_ref, prefix_ref, out_ref, lse_ref):
    mask = allowed_own()
    for kv in range(KV):
        lanes = slice(kv * HS, (kv + 1) * HS)
        vlanes = slice((KV + kv) * HS, (KV + kv + 1) * HS)
        keys = jnp.concatenate([prefix_ref[:, lanes], rk_ref[:, lanes]], axis=0)
        values = jnp.concatenate([prefix_ref[:, vlanes], rv_ref[:, lanes]], axis=0)
        values_t = values.astype(F32).T.astype(BF)
        for g in range(GROUP):
            h = kv * GROUP + g
            cols = slice(h * HS, (h + 1) * HS)
            scores = mm_nt(keys, q_ref[:, cols]) * SCALE
            near = jnp.where(mask, scores[PREFIX:], -1e30)
            scores = jnp.concatenate([scores[:PREFIX], near], axis=0)
            top = jnp.max(scores, axis=0, keepdims=True)
            probs = jnp.exp(scores - top)
            total = jnp.sum(probs, axis=0, keepdims=True)
            low = (probs * (1.0 / total)).astype(BF)
            out_ref[:, cols] = mm(values_t, low).T.astype(BF)
            lse_ref[h : h + 1, :] = top + jnp.log(total)


def project_own_kernel(core_ref, attn_ref, w_ref, resid_ref, xmid_ref):
    part = mm(attn_ref[...], w_ref[...])

    @pl.when(pl.program_id(0) == 0)
    def _():
        xmid_ref[...] = resid_ref[...].astype(F32) + part

    @pl.when(pl.program_id(0) > 0)
    def _():
        xmid_ref[...] += part


def project_kernel(
    core_ref, attn_ref, w_ref, part_ref, gain_ref, router_ref, ids_ref, ids_t_ref,
    xmid_ref, hidden_ref, gates_ref, out_ref, wide,
):
    step = pl.program_id(0)
    part = mm(attn_ref[...], w_ref[...])

    @pl.when(step == 0)
    def _():
        xmid_ref[...] = part_ref[...] + part

    @pl.when(step > 0)
    def _():
        xmid_ref[...] += part

    @pl.when(step == pl.num_programs(0) - 1)
    def _():
        xmid = xmid_ref[...]
        rinv = lax.rsqrt(jnp.mean(xmid * xmid, axis=-1, keepdims=True) + 1e-06)
        hidden = (xmid * rinv * gain_ref[...]).astype(BF)
        hidden_ref[...] = hidden
        select = dispatch_matrix(ids_t_ref[...])
        for n in range(8):
            to_wide(mm(select, hidden[:, n * 256 : (n + 1) * 256]), 2 * n, wide)
        copy_rows(wide, out_ref)
        logits = mm(hidden, router_ref[...])
        chosen = jnp.where(chosen_by_row(ids_ref[...]), jnp.exp(logits), 0.0)
        gates_ref[...] = chosen / jnp.sum(chosen, axis=1, keepdims=True)


def expert_kernel(
    x_hbm, wg_hbm, wu_hbm, wd_hbm, out_hbm, xc_hbm, act_hbm, pg_hbm, pu_hbm,
    wg, wu, wd, xc, act, pg, pu, wide, stage, row_sem, in_sem, out_sem, send_sem,
):
    arrivals = row_copies(x_hbm, stage, row_sem)
    for arrival in arrivals:
        arrival.start()
    loads = [
        pltpu.make_async_copy(src, dst, in_sem.at[i])
        for i, (src, dst) in enumerate(((wg_hbm, wg), (wu_hbm, wu), (wd_hbm, wd)))
    ]
    for load in loads:
        load.start()
    stores = [
        pltpu.make_async_copy(src, dst, out_sem.at[i])
        for i, (src, dst) in enumerate(((xc, xc_hbm), (act, act_hbm), (pg, pg_hbm), (pu, pu_hbm)))
    ]
    from_wide(arrivals, stage, wide, xc)
    stores[0].start()
    loads[0].wait()
    loads[1].wait()

    @pl.loop(0, 3)
    def _(n):
        cols = pl.ds(pl.multiple_of(n * 256, 256), 256)
        gate = mm(xc[...], wg[:, cols])
        up = mm(xc[...], wu[:, cols])
        pg[:, cols] = gate
        pu[:, cols] = up
        act[:, cols] = (gate * jax.nn.sigmoid(gate) * up).astype(BF)

    loads[2].wait()
    departures = row_copies(stage, out_hbm, send_sem)
    send_rows(lambda rows, n: mm(act[rows, :], wd[:, n * 256 : (n + 1) * 256]), stage, wide, departures)
    for store in stores[1:]:
        store.start()
    for store in departures + stores:
        store.wait()


def expert_back_kernel(
    g_hbm, pg_hbm, pu_hbm, wd_hbm, wg_hbm, wu_hbm, back_hbm, ob_hbm, pb_hbm, ub_hbm,
    wd, wg, wu, ob, pb, ub, pg, pu, wide, stage, row_sem, in_sem, out_sem, send_sem,
):
    arrivals = row_copies(g_hbm, stage, row_sem)
    for arrival in arrivals:
        arrival.start()
    loads = [
        pltpu.make_async_copy(src, dst, in_sem.at[i])
        for i, (src, dst) in enumerate(((wd_hbm, wd), (pg_hbm, pg), (pu_hbm, pu), (wg_hbm, wg), (wu_hbm, wu)))
    ]
    for load in loads:
        load.start()
    stores = [
        pltpu.make_async_copy(src, dst, out_sem.at[i])
        for i, (src, dst) in enumerate(((ob, ob_hbm), (pb, pb_hbm), (ub, ub_hbm)))
    ]
    from_wide(arrivals, stage, wide, ob)
    stores[0].start()
    for load in loads[:3]:
        load.wait()

    @pl.loop(0, 3)
    def _(n):
        cols = pl.ds(pl.multiple_of(n * 256, 256), 256)
        act_back = mm_nt(ob[...], wd[cols, :])
        gate = pg[:, cols]
        sig = jax.nn.sigmoid(gate)
        pb[:, cols] = (act_back * pu[:, cols] * (sig * (1.0 + gate * (1.0 - sig)))).astype(BF)
        ub[:, cols] = (act_back * (gate * sig)).astype(BF)

    stores[1].start()
    stores[2].start()
    loads[3].wait()
    loads[4].wait()

    def product(rows, n):
        cols = slice(n * 256, (n + 1) * 256)
        return mm_nt(pb[rows, :], wg[cols, :]) + mm_nt(ub[rows, :], wu[cols, :])

    departures = row_copies(stage, back_hbm, send_sem)
    send_rows(product, stage, wide, departures)
    for store in departures + stores:
        store.wait()


def weight_grad_kernel(xc_ref, ob_ref, act_ref, pb_ref, ub_ref, gate_ref, up_ref, down_ref, act_t):
    @pl.when(pl.program_id(0) == 0)
    def _():
        act_t[...] = act_ref[...].astype(F32).T.astype(BF)

    xt = xc_ref[...].astype(F32).T.astype(BF)
    gate_ref[...] = mm(xt, pb_ref[...]).astype(BF)
    up_ref[...] = mm(xt, ub_ref[...]).astype(BF)
    down_ref[...] = mm(act_t[...], ob_ref[...]).astype(BF)


def owner_kernel(
    rows_hbm, xmid_ref, hidden_ref, gates_ref, grad_ref, live_ref, ids_ref, layer_ref, logit_back_ref, sums_ref,
    wide, stage, rows, row_sem,
):
    arrivals = row_copies(rows_hbm, stage, row_sem)
    for arrival in arrivals:
        arrival.start()
    from_wide(arrivals, stage, wide, rows)
    select = combine_matrix(ids_ref[...])
    grad = jnp.where(live_ref[...] > 0, grad_ref[...].astype(F32), 0.0).astype(BF)
    product = jnp.where(select, mm_nt(grad, rows[...]), 0.0)
    spread = spread_by_slot()
    high, low = split(product)
    gate_back = mm(high, spread) + mm(low, spread)
    gates = gates_ref[...]
    route = gates * (gate_back - jnp.sum(gates * gate_back, axis=1, keepdims=True))
    logit_back = route.astype(BF)
    logit_back_ref[...] = logit_back
    sums_ref[...] = mm_tn(hidden_ref[...], logit_back).astype(BF)
    high, low = split(gates)
    spread = spread_by_expert()
    weight = jnp.where(select, mm(high, spread) + mm(low, spread), 0.0)
    high, low = split(weight)
    for j in range(4):
        cols = slice(j * 512, (j + 1) * 512)
        part = rows[:, cols]
        layer_ref[:, cols] = (xmid_ref[:, cols] + (mm(high, part) + mm(low, part))).astype(BF)


def back_kernel(
    core_ref, rows_hbm, xmid_ref, logit_back_ref, grad_ref, live_ref, ids_ref, gain_ref, router_ref, w_ref, w_other_ref,
    resid_ref, gain_sum_ref, attn_back_ref, acc, wide, stage, rows, row_sem,
):
    @pl.when(pl.program_id(0) == 0)
    def _():
        arrivals = row_copies(rows_hbm, stage, row_sem)
        for arrival in arrivals:
            arrival.start()
        from_wide(arrivals, stage, wide, rows)
        select = to_bf(combine_matrix(ids_ref[...]))
        xmid = xmid_ref[...]
        rinv = lax.rsqrt(jnp.mean(xmid * xmid, axis=-1, keepdims=True) + 1e-06)
        mean = jnp.zeros((ROWS, 1), F32)
        for j in range(4):
            cols = slice(j * 512, (j + 1) * 512)
            value = mm(select, rows[:, cols]) + mm_nt(logit_back_ref[...], router_ref[cols, :])
            normed = xmid[:, cols] * rinv
            partial = jnp.sum(value * normed, axis=0, keepdims=True)
            for c in range(4):
                gain_sum_ref[4 * j + c : 4 * j + c + 1, :] = partial[:, c * 128 : (c + 1) * 128]
            value = value * gain_ref[:, cols]
            acc[:, cols] = value
            mean = mean + jnp.sum(value * normed, axis=-1, keepdims=True)
        mean = mean * (1.0 / D)
        grad = jnp.where(live_ref[...] > 0, grad_ref[...].astype(F32), 0.0)
        resid_ref[...] = (grad + rinv * (acc[...] - xmid * rinv * mean)).astype(BF)

    first = core_ref[0] == 0
    near, far = w_ref[...], w_other_ref[...]
    half = near.shape[0]
    value = mm_nt(resid_ref[...], jnp.concatenate([near, far], axis=0)).astype(BF)

    @pl.when(first)
    def _():
        attn_back_ref[...] = value

    @pl.when(jnp.logical_not(first))
    def _():
        attn_back_ref[:, 0:half] = value[:, half:]
        attn_back_ref[:, half:] = value[:, 0:half]


def attention_back_kernel(q_ref, rk_ref, rv_ref, prefix_ref, lse_ref, ab_ref, dq_ref, dk_ref, dv_ref, dprefix_ref, ds_all, p_all):
    mask = allowed_own()
    for kv in range(KV):
        lanes = slice(kv * HS, (kv + 1) * HS)
        vlanes = slice((KV + kv) * HS, (KV + kv + 1) * HS)
        keys = jnp.concatenate([prefix_ref[:, lanes], rk_ref[:, lanes]], axis=0)
        values = jnp.concatenate([prefix_ref[:, vlanes], rv_ref[:, lanes]], axis=0)
        keys_t = keys.astype(F32).T.astype(BF)
        q_parts = []
        ab_parts = []
        for g in range(GROUP):
            h = kv * GROUP + g
            cols = slice(h * HS, (h + 1) * HS)
            q = q_ref[:, cols]
            ab = ab_ref[:, cols]
            q_parts.append(q)
            ab_parts.append(ab)
            scores = mm_nt(keys, q) * SCALE
            near = jnp.where(mask, scores[PREFIX:], -1e30)
            scores = jnp.concatenate([scores[:PREFIX], near], axis=0)
            probs = jnp.exp(scores - lse_ref[h : h + 1, :])
            prob_back = mm_nt(values, ab)
            delta = jnp.sum(probs * prob_back, axis=0, keepdims=True)
            score_back = (probs * (prob_back - delta) * SCALE).astype(BF)
            at = slice(g * ROWS, (g + 1) * ROWS)
            p_all[:, at] = probs.astype(BF)
            ds_all[:, at] = score_back
            dq_ref[:, cols] = mm(keys_t, score_back).T.astype(BF)
        dk = mm(ds_all[...], jnp.concatenate(q_parts, axis=0)).astype(BF)
        dv = mm(p_all[...], jnp.concatenate(ab_parts, axis=0)).astype(BF)
        dprefix_ref[:, lanes] = dk[:PREFIX]
        dprefix_ref[:, vlanes] = dv[:PREFIX]
        dk_ref[:, lanes] = dk[PREFIX:]
        dv_ref[:, lanes] = dv[PREFIX:]


def struct(shape, dtype):
    return jax.ShapeDtypeStruct(shape, dtype)


def params(limit):
    return pltpu.CompilerParams(vmem_limit_bytes=limit * MIB)


def cost(flops, moved):
    return pl.CostEstimate(flops=int(flops), bytes_accessed=int(moved), transcendentals=0)


VMEM_SPEC = pl.BlockSpec(memory_space=pltpu.VMEM)
ANY_SPEC = pl.BlockSpec(memory_space=pl.ANY)


def whole(shape):
    return pl.BlockSpec(shape, lambda *at: (0,) * len(shape))


def exchange(block):
    moved = lax.all_to_all(
        block.reshape(DEVICES, CAP * PIECES, 128), ("prompt", "resp"), split_axis=0, concat_axis=0, tiled=True
    )
    return moved.reshape(WIDE, 128)


def shards(
    queries, response_keys, response_values, prefix_keys, prompt_values, resid, out_proj, router, norm_gain,
    w_gate, w_up, w_down, expert_ids, lengths, out_grad,
):
    r_at = lax.axis_index("resp")
    ids = expert_ids.reshape(ROWS, TOPK)
    ids_t = ids.T
    live = (jnp.arange(SPAN, dtype=jnp.int32)[None, :] < lengths[0][:, None]).astype(F32).reshape(ROWS, 1)
    grad = out_grad.reshape(ROWS, D)
    q = queries.reshape(ROWS, D)
    rk = response_keys.reshape(ROWS, KV * HS)
    rv = response_values.reshape(ROWS, KV * HS)
    gain = norm_gain.reshape(1, D)

    half = D // N_PROMPT // 2
    core = r_at % 2
    w_own = lax.dynamic_slice(out_proj, (core * half, 0), (half, D))
    w_own = lax.all_gather(w_own, "prompt", axis=0, tiled=True)
    core = core.astype(jnp.int32).reshape(1)

    prefix_part = jnp.concatenate([prefix_keys[0], prompt_values[0]], axis=1)
    prefix = lax.all_to_all(
        jnp.broadcast_to(prefix_part[None], (N_RESP,) + prefix_part.shape), "resp", split_axis=0, concat_axis=0, tiled=True
    ).reshape(PREFIX, 2 * KV * HS)

    attn, lse = pl.pallas_call(
        attention_kernel,
        out_shape=(struct((ROWS, D), BF), struct((HEADS, ROWS), F32)),
        in_specs=[VMEM_SPEC] * 4,
        out_specs=(VMEM_SPEC, VMEM_SPEC),
        compiler_params=params(32),
        cost_estimate=cost(4e9, 2e6),
        name="attention",
    )(q, rk, rv, prefix)
    w_own, attn = lax.optimization_barrier((w_own, attn))
    w_other = lax.ppermute(w_own, "resp", [(i, i ^ 1) for i in range(N_RESP)])

    steps = N_PROMPT
    w_spec = pl.BlockSpec((half, D), lambda i, c: (i, 0))
    xmid = pl.pallas_call(
        project_own_kernel,
        grid_spec=pltpu.PrefetchScalarGridSpec(
            num_scalar_prefetch=1,
            grid=(steps,),
            in_specs=[pl.BlockSpec((ROWS, half), lambda i, c: (0, 2 * i + c[0])), w_spec, whole((ROWS, D))],
            out_specs=whole((ROWS, D)),
        ),
        out_shape=struct((ROWS, D), F32),
        compiler_params=params(32),
        cost_estimate=cost(0.6e9, 6e6),
        name="project_own",
    )(core, attn, w_own, resid.reshape(ROWS, D))
    xmid, hidden, gates, x_rows = pl.pallas_call(
        project_kernel,
        grid_spec=pltpu.PrefetchScalarGridSpec(
            num_scalar_prefetch=1,
            grid=(steps,),
            in_specs=[
                pl.BlockSpec((ROWS, half), lambda i, c: (0, 2 * i + 1 - c[0])), w_spec, whole((ROWS, D)), whole((1, D)), whole((D, EXPERTS)), whole((ROWS, TOPK)), whole((TOPK, ROWS)),
            ],
            out_specs=(
                whole((ROWS, D)), whole((ROWS, D)), whole((ROWS, EXPERTS)), whole((WIDE, 128))
            ),
            scratch_shapes=[pltpu.VMEM((WIDE, 128), F32)],
        ),
        out_shape=(
            struct((ROWS, D), F32), struct((ROWS, D), BF), struct((ROWS, EXPERTS), F32), struct((WIDE, 128), BF),
        ),
        compiler_params=params(40),
        cost_estimate=cost(3e9, 14e6),
        name="project",
    )(core, attn, w_other, xmid, gain, router, ids, ids_t)
    x_rows = exchange(x_rows)

    grad_rows = pl.pallas_call(
        grad_pack_kernel,
        out_shape=struct((WIDE, 128), BF),
        in_specs=[VMEM_SPEC] * 4,
        out_specs=VMEM_SPEC,
        scratch_shapes=[pltpu.VMEM((WIDE, 128), F32)],
        compiler_params=params(32),
        cost_estimate=cost(1.2e9, 4e6),
        name="grad_pack",
    )(ids_t, live, grad, gates)
    x_rows, grad_rows = lax.optimization_barrier((x_rows, grad_rows))
    grad_rows = exchange(grad_rows)

    weights = [pltpu.VMEM((D, FF), BF), pltpu.VMEM((D, FF), BF), pltpu.VMEM((FF, D), BF)]
    wide = [pltpu.VMEM((WIDE, 128), F32), pltpu.VMEM((WIDE, 128), BF)]
    out_rows, xc, act, pg, pu = pl.pallas_call(
        expert_kernel,
        out_shape=(
            struct((WIDE, 128), BF), struct((SLOTS, D), BF), struct((SLOTS, FF), BF), struct((SLOTS, FF), F32),
            struct((SLOTS, FF), F32),
        ),
        in_specs=[ANY_SPEC] * 4,
        out_specs=(ANY_SPEC,) * 5,
        scratch_shapes=weights
        + [
            pltpu.VMEM((SLOTS, D), BF), pltpu.VMEM((SLOTS, FF), BF), pltpu.VMEM((SLOTS, FF), F32),
            pltpu.VMEM((SLOTS, FF), F32),
        ]
        + wide
        + [pltpu.SemaphoreType.DMA((n,)) for n in (BLOCKS, 3, 4, BLOCKS)],
        compiler_params=params(48),
        cost_estimate=cost(8e9, 26e6),
        name="expert",
    )(x_rows, w_gate[0], w_up[0], w_down[0])
    out_rows, grad_rows = lax.optimization_barrier((out_rows, grad_rows))
    out_rows = exchange(out_rows)

    back_rows, ob, pb, ub = pl.pallas_call(
        expert_back_kernel,
        out_shape=(
            struct((WIDE, 128), BF), struct((SLOTS, D), BF), struct((SLOTS, FF), BF), struct((SLOTS, FF), BF)
        ),
        in_specs=[ANY_SPEC] * 6,
        out_specs=(ANY_SPEC,) * 4,
        scratch_shapes=[weights[2], weights[0], weights[1]]
        + [
            pltpu.VMEM((SLOTS, D), BF), pltpu.VMEM((SLOTS, FF), BF), pltpu.VMEM((SLOTS, FF), BF),
            pltpu.VMEM((SLOTS, FF), F32), pltpu.VMEM((SLOTS, FF), F32),
        ]
        + wide
        + [pltpu.SemaphoreType.DMA((n,)) for n in (BLOCKS, 5, 3, BLOCKS)],
        compiler_params=params(48),
        cost_estimate=cost(8e9, 26e6),
        name="expert_back",
    )(grad_rows, pg, pu, w_down[0], w_gate[0], w_up[0])
    back_rows, out_rows = lax.optimization_barrier((back_rows, out_rows))
    back_rows = exchange(back_rows)

    layer_out, logit_back, sums = pl.pallas_call(
        owner_kernel,
        out_shape=(struct((ROWS, D), BF), struct((ROWS, EXPERTS), BF), struct((D, EXPERTS), BF)),
        in_specs=[ANY_SPEC] + [VMEM_SPEC] * 6,
        out_specs=(VMEM_SPEC,) * 3,
        scratch_shapes=wide + [pltpu.VMEM((SLOTS, D), BF), pltpu.SemaphoreType.DMA((BLOCKS,))],
        compiler_params=params(40),
        cost_estimate=cost(3e9, 9e6),
        name="owner",
    )(out_rows, xmid, hidden, gates, grad, live, ids)

    weight_grads = pl.pallas_call(
        weight_grad_kernel,
        grid=(8,),
        out_shape=(struct((D, FF), BF), struct((D, FF), BF), struct((FF, D), BF)),
        in_specs=[
            pl.BlockSpec((SLOTS, 256), lambda i: (0, i)), pl.BlockSpec((SLOTS, 256), lambda i: (0, i)),
            whole((SLOTS, FF)), whole((SLOTS, FF)), whole((SLOTS, FF)),
        ],
        out_specs=(
            pl.BlockSpec((256, FF), lambda i: (i, 0)), pl.BlockSpec((256, FF), lambda i: (i, 0)),
            pl.BlockSpec((FF, 256), lambda i: (0, i)),
        ),
        scratch_shapes=[pltpu.VMEM((FF, SLOTS), BF)],
        compiler_params=params(32),
        cost_estimate=cost(7.3e9, 20e6),
        name="weight_grad",
    )(xc, ob, act, pb, ub)
    back_rows, sums, weight_grads = lax.optimization_barrier((back_rows, sums, weight_grads))
    gate_grad, up_grad, down_grad = weight_grads

    piece = D // DEVICES
    sums = lax.all_to_all(
        sums.reshape(DEVICES, piece, EXPERTS), ("prompt", "resp"), split_axis=0, concat_axis=0, tiled=True
    )

    resid_grad, gain_sum, attn_back = pl.pallas_call(
        back_kernel,
        grid_spec=pltpu.PrefetchScalarGridSpec(
            num_scalar_prefetch=1,
            grid=(steps,),
            in_specs=[
                ANY_SPEC, whole((ROWS, D)), whole((ROWS, EXPERTS)), whole((ROWS, D)), whole((ROWS, 1)),
                whole((ROWS, TOPK)), whole((1, D)), whole((D, EXPERTS)), w_spec, w_spec,
            ],
            out_specs=(whole((ROWS, D)), whole((PIECES, 128)), pl.BlockSpec((ROWS, 2 * half), lambda i, c: (0, i))),
            scratch_shapes=[pltpu.VMEM((ROWS, D), F32)]
            + wide
            + [pltpu.VMEM((SLOTS, D), BF), pltpu.SemaphoreType.DMA((BLOCKS,))],
        ),
        out_shape=(struct((ROWS, D), BF), struct((PIECES, 128), F32), struct((ROWS, D), BF)),
        compiler_params=params(48),
        cost_estimate=cost(3e9, 16e6),
        name="back",
    )(core, back_rows, xmid, logit_back, grad, live, ids, gain, router, w_own, w_other)

    sums = jnp.sum(sums.astype(F32), axis=0)
    sums = jnp.concatenate([sums, gain_sum], axis=0).astype(BF)
    sums = lax.all_to_all(
        jnp.broadcast_to(sums[None], (DEVICES, piece + PIECES, EXPERTS)),
        ("prompt", "resp"), split_axis=0, concat_axis=0, tiled=True,
    ).astype(F32)
    router_grad = sums[:, :piece].reshape(D, EXPERTS)
    gain_grad = jnp.sum(sums[:, piece:], axis=0).reshape(D)

    query_grad, resp_key_grad, resp_value_grad, prefix_grad = pl.pallas_call(
        attention_back_kernel,
        out_shape=(
            struct((ROWS, D), BF), struct((ROWS, KV * HS), BF), struct((ROWS, KV * HS), BF),
            struct((PREFIX, 2 * KV * HS), BF),
        ),
        in_specs=[VMEM_SPEC] * 6,
        out_specs=(VMEM_SPEC,) * 4,
        scratch_shapes=[pltpu.VMEM((PREFIX + ROWS, GROUP * ROWS), BF)] * 2,
        compiler_params=params(32),
        cost_estimate=cost(8e9, 4e6),
        name="attention_back",
    )(q, rk, rv, prefix, lse, attn_back)

    prefix_grad = lax.all_to_all(
        prefix_grad.reshape(N_RESP, SHARE, 2 * KV * HS), "resp", split_axis=0, concat_axis=0, tiled=True
    )
    prefix_grad = jnp.sum(prefix_grad.astype(F32), axis=0).astype(BF)

    rows_shape = (1, ROWS // SPAN, SPAN, D)
    near_shape = (1, ROWS // SPAN, SPAN, KV * HS)
    return (
        layer_out.reshape(rows_shape),
        resid_grad.reshape(rows_shape),
        query_grad.reshape(rows_shape),
        resp_key_grad.reshape(near_shape),
        resp_value_grad.reshape(near_shape),
        prefix_grad[None, :, : KV * HS],
        prefix_grad[None, :, KV * HS :],
        router_grad,
        gain_grad,
        gate_grad[None],
        up_grad[None],
        down_grad[None],
    )


def solution(mesh):
    in_specs = (
        P("prompt", "resp", None, None),
        P("prompt", "resp", None, None),
        P("prompt", "resp", None, None),
        P("prompt", "resp", None),
        P("prompt", "resp", None),
        P("prompt", "resp", None, None),
        P("prompt", None),
        P(),
        P(),
        P(("prompt", "resp"), None, None),
        P(("prompt", "resp"), None, None),
        P(("prompt", "resp"), None, None),
        P("prompt", "resp", None, None),
        P("prompt", "resp"),
        P("prompt", "resp", None, None),
    )
    out_specs = (
        P("prompt", "resp", None, None),
        P("prompt", "resp", None, None),
        P("prompt", "resp", None, None),
        P("prompt", "resp", None, None),
        P("prompt", "resp", None, None),
        P("prompt", "resp", None),
        P("prompt", "resp", None),
        P(),
        P(),
        P(("prompt", "resp"), None, None),
        P(("prompt", "resp"), None, None),
        P(("prompt", "resp"), None, None),
    )
    return jax.shard_map(shards, mesh=mesh, in_specs=in_specs, out_specs=out_specs, check_vma=False)
```

```python
import jax
import jax.numpy as jnp
from jax import lax
from jax.experimental import pallas as pl
from jax.experimental.pallas import tpu as pltpu
from jax.sharding import PartitionSpec as P

D = 2048
HEADS = 16
KV = 2
GROUP = HEADS // KV
HS = 128
FF = 768
TOPK = 4
PREFIX = 512
SPAN = 64
ROWS = 128
EXPERTS = 128
CAP = 6
N_PROMPT = 8
N_RESP = 16
DEVICES = 128
SLOTS = DEVICES * CAP
SHARE = PREFIX // N_RESP
BLOCKS = 3
BLOCK = SLOTS // BLOCKS
PIECES = D // 128
WIDE = SLOTS * PIECES
SCALE = HS ** (-0.5)
BF = jnp.bfloat16
F32 = jnp.float32
MIB = 1024 * 1024


def mm(a, b):
    return jnp.dot(a, b, preferred_element_type=F32)


def mm_nt(a, b):
    return lax.dot_general(a, b, (((1,), (1,)), ((), ())), preferred_element_type=F32)


def mm_tn(a, b):
    return lax.dot_general(a, b, (((0,), (0,)), ((), ())), preferred_element_type=F32)


def iota(shape, dim):
    return lax.broadcasted_iota(jnp.int32, shape, dim)


def chosen_by_row(ids):
    lanes = iota((ROWS, EXPERTS), 1)
    hit = ids[:, 0:1] == lanes
    for k in range(1, TOPK):
        hit = hit | (ids[:, k : k + 1] == lanes)
    return hit


def chosen_by_expert(ids_t):
    subs = iota((EXPERTS, ROWS), 0)
    hit = ids_t[0:1, :] == subs
    for k in range(1, TOPK):
        hit = hit | (ids_t[k : k + 1, :] == subs)
    return hit


def to_bf(mask):
    return jnp.where(mask, 1.0, 0.0).astype(BF)


def expert_of(slot):
    return (slot * 43691) >> 18


def spread_by_slot():
    return to_bf(expert_of(iota((SLOTS, EXPERTS), 0)) == iota((SLOTS, EXPERTS), 1))


def spread_by_expert():
    return to_bf(expert_of(iota((EXPERTS, SLOTS), 1)) == iota((EXPERTS, SLOTS), 0))


def slots_by_expert(ids_t):
    hit = chosen_by_expert(ids_t)
    before = to_bf(iota((ROWS, ROWS), 0) < iota((ROWS, ROWS), 1))
    return jnp.where(hit, mm(to_bf(hit), before), -1.0)


def dispatch_matrix(ids_t):
    slot = mm(spread_by_slot(), slots_by_expert(ids_t).astype(BF)).astype(jnp.int32)
    at = iota((SLOTS, ROWS), 0)
    return to_bf(slot == at - expert_of(at) * CAP)


def combine_matrix(ids):
    hit = chosen_by_row(ids)
    before = to_bf(iota((ROWS, ROWS), 1) < iota((ROWS, ROWS), 0))
    slot = jnp.where(hit, mm(before, to_bf(hit)), -1.0).astype(BF)
    slot = mm(slot, spread_by_expert()).astype(jnp.int32)
    at = iota((ROWS, SLOTS), 1)
    return slot == at - expert_of(at) * CAP


def row_copies(src, dst, sems):
    step = BLOCK * PIECES
    return [
        pltpu.make_async_copy(src.at[pl.ds(m * step, step)], dst.at[pl.ds(m * step, step)], sems.at[m])
        for m in range(BLOCKS)
    ]


def from_wide(copies, stage, wide, dst):
    step = BLOCK * PIECES
    for m in range(BLOCKS):
        copies[m].wait()

        @pl.loop(0, 4)
        def _(i):
            rows = pl.ds(pl.multiple_of(m * step + i * (step // 4), step // 4), step // 4)
            wide[rows, :] = stage[rows, :].astype(F32)

        at = slice(m * BLOCK, (m + 1) * BLOCK)
        for c in range(PIECES):
            part = wide[pl.ds(m * step + c, BLOCK, stride=PIECES), :]
            dst[at, c * 128 : (c + 1) * 128] = part.astype(BF)


def send_rows(product, stage, wide, copies):
    step = BLOCK * PIECES
    for m in range(BLOCKS):
        rows = slice(m * BLOCK, (m + 1) * BLOCK)
        for n in range(8):
            value = product(rows, n)
            for c in range(2):
                wide[pl.ds(m * step + 2 * n + c, BLOCK, stride=PIECES), :] = value[:, c * 128 : (c + 1) * 128]

        @pl.loop(0, 4)
        def _(i):
            part = pl.ds(pl.multiple_of(m * step + i * (step // 4), step // 4), step // 4)
            stage[part, :] = wide[part, :].astype(BF)

        copies[m].start()


def split(value):
    high = value.astype(BF)
    return high, (value - high.astype(F32)).astype(BF)


def grad_pack_kernel(
    ids_t_ref, ids_ref, live_ref, grad_ref, hidden_ref, router_ref, gates_ref, out_hbm, wide, stage, send_sem
):
    logits = mm(hidden_ref[...], router_ref[...])
    chosen = jnp.where(chosen_by_row(ids_ref[...]), jnp.exp(logits), 0.0)
    gates = chosen / jnp.sum(chosen, axis=1, keepdims=True)
    gates_ref[...] = gates
    select = dispatch_matrix(ids_t_ref[...])
    high, low = split(gates)
    mine = expert_of(iota((SLOTS, EXPERTS), 0)) == iota((SLOTS, EXPERTS), 1)
    scale = jnp.sum(jnp.where(mine, mm(select, high) + mm(select, low), 0.0), axis=1, keepdims=True)
    grad = jnp.where(live_ref[...] > 0, grad_ref[...].astype(F32), 0.0).astype(BF)
    departures = row_copies(stage, out_hbm, send_sem)
    send_rows(
        lambda rows, n: scale[rows] * mm(select[rows], grad[:, n * 256 : (n + 1) * 256]), stage, wide, departures
    )
    for departure in departures:
        departure.wait()


def allowed_own():
    key = iota((ROWS, ROWS), 0)
    row = iota((ROWS, ROWS), 1)
    return ((key >> 6) == (row >> 6)) & ((key & 63) <= (row & 63))


def attention_kernel(q_ref, rk_ref, rv_ref, prefix_ref, out_ref, lse_ref):
    mask = allowed_own()
    for kv in range(KV):
        lanes = slice(kv * HS, (kv + 1) * HS)
        vlanes = slice((KV + kv) * HS, (KV + kv + 1) * HS)
        keys = jnp.concatenate([prefix_ref[:, lanes], rk_ref[:, lanes]], axis=0)
        values = jnp.concatenate([prefix_ref[:, vlanes], rv_ref[:, lanes]], axis=0)
        values_t = values.astype(F32).T.astype(BF)
        for g in range(GROUP):
            h = kv * GROUP + g
            cols = slice(h * HS, (h + 1) * HS)
            scores = mm_nt(keys, q_ref[:, cols]) * SCALE
            near = jnp.where(mask, scores[PREFIX:], -1e30)
            scores = jnp.concatenate([scores[:PREFIX], near], axis=0)
            top = jnp.max(scores, axis=0, keepdims=True)
            probs = jnp.exp(scores - top)
            total = jnp.sum(probs, axis=0, keepdims=True)
            low = (probs * (1.0 / total)).astype(BF)
            out_ref[:, cols] = mm(values_t, low).T.astype(BF)
            lse_ref[h : h + 1, :] = top + jnp.log(total)


def project_own_kernel(core_ref, attn_a_ref, attn_b_ref, w_ref, resid_ref, xmid_ref):
    part = mm(jnp.concatenate([attn_a_ref[...], attn_b_ref[...]], axis=1), w_ref[...])

    @pl.when(pl.program_id(0) == 0)
    def _():
        xmid_ref[...] = resid_ref[...].astype(F32) + part

    @pl.when(pl.program_id(0) > 0)
    def _():
        xmid_ref[...] += part


def project_kernel(
    core_ref, attn_a_ref, attn_b_ref, w_ref, part_ref, gain_ref, ids_t_ref,
    xmid_ref, hidden_ref, out_hbm, wide, stage, send_sem,
):
    step = pl.program_id(0)
    part = mm(jnp.concatenate([attn_a_ref[...], attn_b_ref[...]], axis=1), w_ref[...])

    @pl.when(step == 0)
    def _():
        xmid_ref[...] = part_ref[...] + part

    @pl.when(step > 0)
    def _():
        xmid_ref[...] += part

    @pl.when(step == pl.num_programs(0) - 1)
    def _():
        xmid = xmid_ref[...]
        rinv = lax.rsqrt(jnp.mean(xmid * xmid, axis=-1, keepdims=True) + 1e-06)
        hidden = (xmid * rinv * gain_ref[...]).astype(BF)
        hidden_ref[...] = hidden
        select = dispatch_matrix(ids_t_ref[...])
        departures = row_copies(stage, out_hbm, send_sem)
        send_rows(lambda rows, n: mm(select[rows], hidden[:, n * 256 : (n + 1) * 256]), stage, wide, departures)
        for departure in departures:
            departure.wait()


def expert_kernel(
    x_hbm, wg_hbm, wu_hbm, wd_hbm, out_hbm, xc_hbm, act_hbm, pg_hbm, pu_hbm,
    wg, wu, wd, xc, act, pg, pu, wide, stage, row_sem, in_sem, out_sem, send_sem,
):
    arrivals = row_copies(x_hbm, stage, row_sem)
    for arrival in arrivals:
        arrival.start()
    loads = [
        pltpu.make_async_copy(src, dst, in_sem.at[i])
        for i, (src, dst) in enumerate(((wg_hbm, wg), (wu_hbm, wu), (wd_hbm, wd)))
    ]
    for load in loads:
        load.start()
    stores = [
        pltpu.make_async_copy(src, dst, out_sem.at[i])
        for i, (src, dst) in enumerate(((xc, xc_hbm), (act, act_hbm), (pg, pg_hbm), (pu, pu_hbm)))
    ]
    from_wide(arrivals, stage, wide, xc)
    stores[0].start()
    loads[0].wait()
    loads[1].wait()

    @pl.loop(0, 3)
    def _(n):
        cols = pl.ds(pl.multiple_of(n * 256, 256), 256)
        gate = mm(xc[...], wg[:, cols])
        up = mm(xc[...], wu[:, cols])
        pg[:, cols] = gate
        pu[:, cols] = up
        act[:, cols] = (gate * jax.nn.sigmoid(gate) * up).astype(BF)

    loads[2].wait()
    departures = row_copies(stage, out_hbm, send_sem)
    send_rows(lambda rows, n: mm(act[rows, :], wd[:, n * 256 : (n + 1) * 256]), stage, wide, departures)
    for store in stores[1:]:
        store.start()
    for store in departures + stores:
        store.wait()


def expert_back_kernel(
    g_hbm, pg_hbm, pu_hbm, wd_hbm, wg_hbm, wu_hbm, back_hbm, ob_hbm, pb_hbm, ub_hbm,
    wd, wg, wu, ob, pb, ub, pg, pu, wide, stage, row_sem, in_sem, out_sem, send_sem,
):
    arrivals = row_copies(g_hbm, stage, row_sem)
    for arrival in arrivals:
        arrival.start()
    loads = [
        pltpu.make_async_copy(src, dst, in_sem.at[i])
        for i, (src, dst) in enumerate(((wd_hbm, wd), (pg_hbm, pg), (pu_hbm, pu), (wg_hbm, wg), (wu_hbm, wu)))
    ]
    for load in loads:
        load.start()
    stores = [
        pltpu.make_async_copy(src, dst, out_sem.at[i])
        for i, (src, dst) in enumerate(((ob, ob_hbm), (pb, pb_hbm), (ub, ub_hbm)))
    ]
    from_wide(arrivals, stage, wide, ob)
    stores[0].start()
    for load in loads[:3]:
        load.wait()

    @pl.loop(0, 3)
    def _(n):
        cols = pl.ds(pl.multiple_of(n * 256, 256), 256)
        act_back = mm_nt(ob[...], wd[cols, :])
        gate = pg[:, cols]
        sig = jax.nn.sigmoid(gate)
        pb[:, cols] = (act_back * pu[:, cols] * (sig * (1.0 + gate * (1.0 - sig)))).astype(BF)
        ub[:, cols] = (act_back * (gate * sig)).astype(BF)

    stores[1].start()
    stores[2].start()
    loads[3].wait()
    loads[4].wait()

    def product(rows, n):
        cols = slice(n * 256, (n + 1) * 256)
        return mm_nt(pb[rows, :], wg[cols, :]) + mm_nt(ub[rows, :], wu[cols, :])

    departures = row_copies(stage, back_hbm, send_sem)
    send_rows(product, stage, wide, departures)
    for store in departures + stores:
        store.wait()


def weight_grad_kernel(xc_ref, ob_ref, act_ref, pb_ref, ub_ref, gate_ref, up_ref, down_ref, act_t):
    @pl.when(pl.program_id(0) == 0)
    def _():
        act_t[...] = act_ref[...].astype(F32).T.astype(BF)

    xt = xc_ref[...].astype(F32).T.astype(BF)
    gate_ref[...] = mm(xt, pb_ref[...]).astype(BF)
    up_ref[...] = mm(xt, ub_ref[...]).astype(BF)
    down_ref[...] = mm(act_t[...], ob_ref[...]).astype(BF)


def owner_kernel(
    rows_hbm, xmid_ref, hidden_ref, gates_ref, grad_ref, live_ref, ids_ref, layer_ref, logit_back_ref, sums_ref,
    wide, stage, rows, row_sem,
):
    arrivals = row_copies(rows_hbm, stage, row_sem)
    for arrival in arrivals:
        arrival.start()
    from_wide(arrivals, stage, wide, rows)
    select = combine_matrix(ids_ref[...])
    grad = jnp.where(live_ref[...] > 0, grad_ref[...].astype(F32), 0.0).astype(BF)
    product = jnp.where(select, mm_nt(grad, rows[...]), 0.0)
    spread = spread_by_slot()
    high, low = split(product)
    gate_back = mm(high, spread) + mm(low, spread)
    gates = gates_ref[...]
    route = gates * (gate_back - jnp.sum(gates * gate_back, axis=1, keepdims=True))
    logit_back = route.astype(BF)
    logit_back_ref[...] = logit_back
    sums_ref[...] = mm_tn(hidden_ref[...], logit_back).astype(BF)
    high, low = split(gates)
    spread = spread_by_expert()
    weight = jnp.where(select, mm(high, spread) + mm(low, spread), 0.0)
    high, low = split(weight)
    for j in range(4):
        cols = slice(j * 512, (j + 1) * 512)
        part = rows[:, cols]
        layer_ref[:, cols] = (xmid_ref[:, cols] + (mm(high, part) + mm(low, part))).astype(BF)


def back_kernel(
    core_ref, rows_hbm, xmid_ref, logit_back_ref, grad_ref, live_ref, ids_ref, gain_ref, router_ref, w_ref, w_other_ref,
    resid_ref, gain_sum_ref, attn_back_ref, acc, wide, stage, rows, row_sem,
):
    @pl.when(pl.program_id(0) == 0)
    def _():
        arrivals = row_copies(rows_hbm, stage, row_sem)
        for arrival in arrivals:
            arrival.start()
        from_wide(arrivals, stage, wide, rows)
        select = to_bf(combine_matrix(ids_ref[...]))
        xmid = xmid_ref[...]
        rinv = lax.rsqrt(jnp.mean(xmid * xmid, axis=-1, keepdims=True) + 1e-06)
        mean = jnp.zeros((ROWS, 1), F32)
        for j in range(4):
            cols = slice(j * 512, (j + 1) * 512)
            value = mm(select, rows[:, cols]) + mm_nt(logit_back_ref[...], router_ref[cols, :])
            normed = xmid[:, cols] * rinv
            partial = jnp.sum(value * normed, axis=0, keepdims=True)
            for c in range(4):
                gain_sum_ref[4 * j + c : 4 * j + c + 1, :] = partial[:, c * 128 : (c + 1) * 128]
            value = value * gain_ref[:, cols]
            acc[:, cols] = value
            mean = mean + jnp.sum(value * normed, axis=-1, keepdims=True)
        mean = mean * (1.0 / D)
        grad = jnp.where(live_ref[...] > 0, grad_ref[...].astype(F32), 0.0)
        resid_ref[...] = (grad + rinv * (acc[...] - xmid * rinv * mean)).astype(BF)

    half = D // N_PROMPT // 2
    near = [w_ref[0:half, :], w_ref[half:, :]]
    far = [w_other_ref[0:half, :], w_other_ref[half:, :]]

    def attn_back(first, second):
        rows = jnp.concatenate([first[0], second[0], first[1], second[1]], axis=0)
        attn_back_ref[...] = mm_nt(resid_ref[...], rows).astype(BF)

    @pl.when(core_ref[0] == 0)
    def _():
        attn_back(near, far)

    @pl.when(core_ref[0] != 0)
    def _():
        attn_back(far, near)


def attention_back_kernel(q_ref, rk_ref, rv_ref, prefix_ref, lse_ref, ab_ref, dq_ref, dk_ref, dv_ref, dprefix_ref, ds_all, p_all):
    mask = allowed_own()
    for kv in range(KV):
        lanes = slice(kv * HS, (kv + 1) * HS)
        vlanes = slice((KV + kv) * HS, (KV + kv + 1) * HS)
        keys = jnp.concatenate([prefix_ref[:, lanes], rk_ref[:, lanes]], axis=0)
        values = jnp.concatenate([prefix_ref[:, vlanes], rv_ref[:, lanes]], axis=0)
        keys_t = keys.astype(F32).T.astype(BF)
        q_parts = []
        ab_parts = []
        for g in range(GROUP):
            h = kv * GROUP + g
            cols = slice(h * HS, (h + 1) * HS)
            q = q_ref[:, cols]
            ab = ab_ref[:, cols]
            q_parts.append(q)
            ab_parts.append(ab)
            scores = mm_nt(keys, q) * SCALE
            near = jnp.where(mask, scores[PREFIX:], -1e30)
            scores = jnp.concatenate([scores[:PREFIX], near], axis=0)
            probs = jnp.exp(scores - lse_ref[h : h + 1, :])
            prob_back = mm_nt(values, ab)
            delta = jnp.sum(probs * prob_back, axis=0, keepdims=True)
            score_back = (probs * (prob_back - delta) * SCALE).astype(BF)
            at = slice(g * ROWS, (g + 1) * ROWS)
            p_all[:, at] = probs.astype(BF)
            ds_all[:, at] = score_back
            dq_ref[:, cols] = mm(keys_t, score_back).T.astype(BF)
        dk = mm(ds_all[...], jnp.concatenate(q_parts, axis=0)).astype(BF)
        dv = mm(p_all[...], jnp.concatenate(ab_parts, axis=0)).astype(BF)
        dprefix_ref[:, lanes] = dk[:PREFIX]
        dprefix_ref[:, vlanes] = dv[:PREFIX]
        dk_ref[:, lanes] = dk[PREFIX:]
        dv_ref[:, lanes] = dv[PREFIX:]


def struct(shape, dtype):
    return jax.ShapeDtypeStruct(shape, dtype)


def params(limit):
    return pltpu.CompilerParams(vmem_limit_bytes=limit * MIB)


def cost(flops, moved):
    return pl.CostEstimate(flops=int(flops), bytes_accessed=int(moved), transcendentals=0)


VMEM_SPEC = pl.BlockSpec(memory_space=pltpu.VMEM)
ANY_SPEC = pl.BlockSpec(memory_space=pl.ANY)


def whole(shape):
    return pl.BlockSpec(shape, lambda *at: (0,) * len(shape))


def exchange(block):
    moved = lax.all_to_all(
        block.reshape(DEVICES, CAP * PIECES, 128), ("prompt", "resp"), split_axis=0, concat_axis=0, tiled=True
    )
    return moved.reshape(WIDE, 128)


def shards(
    queries, response_keys, response_values, prefix_keys, prompt_values, resid, out_proj, router, norm_gain,
    w_gate, w_up, w_down, expert_ids, lengths, out_grad,
):
    r_at = lax.axis_index("resp")
    ids = expert_ids.reshape(ROWS, TOPK)
    ids_t = ids.T
    live = (jnp.arange(SPAN, dtype=jnp.int32)[None, :] < lengths[0][:, None]).astype(F32).reshape(ROWS, 1)
    grad = out_grad.reshape(ROWS, D)
    q = queries.reshape(ROWS, D)
    rk = response_keys.reshape(ROWS, KV * HS)
    rv = response_values.reshape(ROWS, KV * HS)
    gain = norm_gain.reshape(1, D)

    half = D // N_PROMPT // 2
    core = r_at % 2
    w_own = lax.dynamic_slice(out_proj, (core * half, 0), (half, D))
    w_own = lax.all_gather(w_own, "prompt", axis=0, tiled=True)
    core = core.astype(jnp.int32).reshape(1)

    prefix_part = jnp.concatenate([prefix_keys[0], prompt_values[0]], axis=1)
    prefix = lax.all_to_all(
        jnp.broadcast_to(prefix_part[None], (N_RESP,) + prefix_part.shape), "resp", split_axis=0, concat_axis=0, tiled=True
    ).reshape(PREFIX, 2 * KV * HS)

    attn, lse = pl.pallas_call(
        attention_kernel,
        out_shape=(struct((ROWS, D), BF), struct((HEADS, ROWS), F32)),
        in_specs=[VMEM_SPEC] * 4,
        out_specs=(VMEM_SPEC, VMEM_SPEC),
        compiler_params=params(32),
        cost_estimate=cost(4e9, 2e6),
        name="attention",
    )(q, rk, rv, prefix)
    w_own, attn = lax.optimization_barrier((w_own, attn))
    w_other = lax.ppermute(w_own, "resp", [(i, i ^ 1) for i in range(N_RESP)])

    steps = N_PROMPT // 2
    w_spec = pl.BlockSpec((2 * half, D), lambda i, c: (i, 0))
    xmid = pl.pallas_call(
        project_own_kernel,
        grid_spec=pltpu.PrefetchScalarGridSpec(
            num_scalar_prefetch=1,
            grid=(steps,),
            in_specs=[
                pl.BlockSpec((ROWS, half), lambda i, c: (0, 4 * i + c[0])),
                pl.BlockSpec((ROWS, half), lambda i, c: (0, 4 * i + 2 + c[0])),
                w_spec, whole((ROWS, D)),
            ],
            out_specs=whole((ROWS, D)),
        ),
        out_shape=struct((ROWS, D), F32),
        compiler_params=params(32),
        cost_estimate=cost(0.6e9, 6e6),
        name="project_own",
    )(core, attn, attn, w_own, resid.reshape(ROWS, D))
    rows_scratch = [pltpu.VMEM((WIDE, 128), F32), pltpu.VMEM((WIDE, 128), BF), pltpu.SemaphoreType.DMA((BLOCKS,))]
    xmid, hidden, x_rows = pl.pallas_call(
        project_kernel,
        grid_spec=pltpu.PrefetchScalarGridSpec(
            num_scalar_prefetch=1,
            grid=(steps,),
            in_specs=[
                pl.BlockSpec((ROWS, half), lambda i, c: (0, 4 * i + 1 - c[0])),
                pl.BlockSpec((ROWS, half), lambda i, c: (0, 4 * i + 3 - c[0])),
                w_spec, whole((ROWS, D)), whole((1, D)), whole((TOPK, ROWS)),
            ],
            out_specs=(whole((ROWS, D)), whole((ROWS, D)), ANY_SPEC),
            scratch_shapes=rows_scratch,
        ),
        out_shape=(struct((ROWS, D), F32), struct((ROWS, D), BF), struct((WIDE, 128), BF)),
        compiler_params=params(40),
        cost_estimate=cost(3e9, 14e6),
        name="project",
    )(core, attn, attn, w_other, xmid, gain, ids_t)
    x_rows = exchange(x_rows)

    gates, grad_rows = pl.pallas_call(
        grad_pack_kernel,
        out_shape=(struct((ROWS, EXPERTS), F32), struct((WIDE, 128), BF)),
        in_specs=[VMEM_SPEC] * 6,
        out_specs=(VMEM_SPEC, ANY_SPEC),
        scratch_shapes=rows_scratch,
        compiler_params=params(32),
        cost_estimate=cost(1.2e9, 4e6),
        name="grad_pack",
    )(ids_t, ids, live, grad, hidden, router)
    x_rows, grad_rows = lax.optimization_barrier((x_rows, grad_rows))
    grad_rows = exchange(grad_rows)

    weights = [pltpu.VMEM((D, FF), BF), pltpu.VMEM((D, FF), BF), pltpu.VMEM((FF, D), BF)]
    wide = [pltpu.VMEM((WIDE, 128), F32), pltpu.VMEM((WIDE, 128), BF)]
    out_rows, xc, act, pg, pu = pl.pallas_call(
        expert_kernel,
        out_shape=(
            struct((WIDE, 128), BF), struct((SLOTS, D), BF), struct((SLOTS, FF), BF), struct((SLOTS, FF), F32),
            struct((SLOTS, FF), F32),
        ),
        in_specs=[ANY_SPEC] * 4,
        out_specs=(ANY_SPEC,) * 5,
        scratch_shapes=weights
        + [
            pltpu.VMEM((SLOTS, D), BF), pltpu.VMEM((SLOTS, FF), BF), pltpu.VMEM((SLOTS, FF), F32),
            pltpu.VMEM((SLOTS, FF), F32),
        ]
        + wide
        + [pltpu.SemaphoreType.DMA((n,)) for n in (BLOCKS, 3, 4, BLOCKS)],
        compiler_params=params(48),
        cost_estimate=cost(8e9, 26e6),
        name="expert",
    )(x_rows, w_gate[0], w_up[0], w_down[0])
    out_rows, grad_rows = lax.optimization_barrier((out_rows, grad_rows))
    out_rows = exchange(out_rows)

    back_rows, ob, pb, ub = pl.pallas_call(
        expert_back_kernel,
        out_shape=(
            struct((WIDE, 128), BF), struct((SLOTS, D), BF), struct((SLOTS, FF), BF), struct((SLOTS, FF), BF)
        ),
        in_specs=[ANY_SPEC] * 6,
        out_specs=(ANY_SPEC,) * 4,
        scratch_shapes=[weights[2], weights[0], weights[1]]
        + [
            pltpu.VMEM((SLOTS, D), BF), pltpu.VMEM((SLOTS, FF), BF), pltpu.VMEM((SLOTS, FF), BF),
            pltpu.VMEM((SLOTS, FF), F32), pltpu.VMEM((SLOTS, FF), F32),
        ]
        + wide
        + [pltpu.SemaphoreType.DMA((n,)) for n in (BLOCKS, 5, 3, BLOCKS)],
        compiler_params=params(48),
        cost_estimate=cost(8e9, 26e6),
        name="expert_back",
    )(grad_rows, pg, pu, w_down[0], w_gate[0], w_up[0])
    back_rows, out_rows = lax.optimization_barrier((back_rows, out_rows))
    back_rows = exchange(back_rows)

    layer_out, logit_back, sums = pl.pallas_call(
        owner_kernel,
        out_shape=(struct((ROWS, D), BF), struct((ROWS, EXPERTS), BF), struct((D, EXPERTS), BF)),
        in_specs=[ANY_SPEC] + [VMEM_SPEC] * 6,
        out_specs=(VMEM_SPEC,) * 3,
        scratch_shapes=wide + [pltpu.VMEM((SLOTS, D), BF), pltpu.SemaphoreType.DMA((BLOCKS,))],
        compiler_params=params(40),
        cost_estimate=cost(3e9, 9e6),
        name="owner",
    )(out_rows, xmid, hidden, gates, grad, live, ids)

    weight_grads = pl.pallas_call(
        weight_grad_kernel,
        grid=(8,),
        out_shape=(struct((D, FF), BF), struct((D, FF), BF), struct((FF, D), BF)),
        in_specs=[
            pl.BlockSpec((SLOTS, 256), lambda i: (0, i)), pl.BlockSpec((SLOTS, 256), lambda i: (0, i)),
            whole((SLOTS, FF)), whole((SLOTS, FF)), whole((SLOTS, FF)),
        ],
        out_specs=(
            pl.BlockSpec((256, FF), lambda i: (i, 0)), pl.BlockSpec((256, FF), lambda i: (i, 0)),
            pl.BlockSpec((FF, 256), lambda i: (0, i)),
        ),
        scratch_shapes=[pltpu.VMEM((FF, SLOTS), BF)],
        compiler_params=params(32),
        cost_estimate=cost(7.3e9, 20e6),
        name="weight_grad",
    )(xc, ob, act, pb, ub)
    back_rows, sums, weight_grads = lax.optimization_barrier((back_rows, sums, weight_grads))
    gate_grad, up_grad, down_grad = weight_grads

    piece = D // DEVICES
    sums = lax.all_to_all(
        sums.reshape(DEVICES, piece, EXPERTS), ("prompt", "resp"), split_axis=0, concat_axis=0, tiled=True
    )

    resid_grad, gain_sum, attn_back = pl.pallas_call(
        back_kernel,
        grid_spec=pltpu.PrefetchScalarGridSpec(
            num_scalar_prefetch=1,
            grid=(steps,),
            in_specs=[
                ANY_SPEC, whole((ROWS, D)), whole((ROWS, EXPERTS)), whole((ROWS, D)), whole((ROWS, 1)),
                whole((ROWS, TOPK)), whole((1, D)), whole((D, EXPERTS)), w_spec, w_spec,
            ],
            out_specs=(whole((ROWS, D)), whole((PIECES, 128)), pl.BlockSpec((ROWS, 4 * half), lambda i, c: (0, i))),
            scratch_shapes=[pltpu.VMEM((ROWS, D), F32)]
            + wide
            + [pltpu.VMEM((SLOTS, D), BF), pltpu.SemaphoreType.DMA((BLOCKS,))],
        ),
        out_shape=(struct((ROWS, D), BF), struct((PIECES, 128), F32), struct((ROWS, D), BF)),
        compiler_params=params(48),
        cost_estimate=cost(3e9, 16e6),
        name="back",
    )(core, back_rows, xmid, logit_back, grad, live, ids, gain, router, w_own, w_other)

    sums = jnp.sum(sums.astype(F32), axis=0)
    sums = jnp.concatenate([sums, gain_sum], axis=0).astype(BF)
    sums = lax.all_to_all(
        jnp.broadcast_to(sums[None], (DEVICES, piece + PIECES, EXPERTS)),
        ("prompt", "resp"), split_axis=0, concat_axis=0, tiled=True,
    )

    query_grad, resp_key_grad, resp_value_grad, prefix_grad = pl.pallas_call(
        attention_back_kernel,
        out_shape=(
            struct((ROWS, D), BF), struct((ROWS, KV * HS), BF), struct((ROWS, KV * HS), BF),
            struct((PREFIX, 2 * KV * HS), BF),
        ),
        in_specs=[VMEM_SPEC] * 6,
        out_specs=(VMEM_SPEC,) * 4,
        scratch_shapes=[pltpu.VMEM((PREFIX + ROWS, GROUP * ROWS), BF)] * 2,
        compiler_params=params(32),
        cost_estimate=cost(8e9, 4e6),
        name="attention_back",
    )(q, rk, rv, prefix, lse, attn_back)

    prefix_grad, sums = lax.optimization_barrier((prefix_grad, sums))
    sums = sums.astype(F32)
    router_grad = sums[:, :piece].reshape(D, EXPERTS)
    gain_grad = jnp.sum(sums[:, piece:], axis=0).reshape(D)

    prefix_grad = lax.all_to_all(
        prefix_grad.reshape(N_RESP, SHARE, 2 * KV * HS), "resp", split_axis=0, concat_axis=0, tiled=True
    )
    prefix_grad = jnp.sum(prefix_grad.astype(F32), axis=0).astype(BF)

    rows_shape = (1, ROWS // SPAN, SPAN, D)
    near_shape = (1, ROWS // SPAN, SPAN, KV * HS)
    return (
        layer_out.reshape(rows_shape),
        resid_grad.reshape(rows_shape),
        query_grad.reshape(rows_shape),
        resp_key_grad.reshape(near_shape),
        resp_value_grad.reshape(near_shape),
        prefix_grad[None, :, : KV * HS],
        prefix_grad[None, :, KV * HS :],
        router_grad,
        gain_grad,
        gate_grad[None],
        up_grad[None],
        down_grad[None],
    )


def solution(mesh):
    in_specs = (
        P("prompt", "resp", None, None),
        P("prompt", "resp", None, None),
        P("prompt", "resp", None, None),
        P("prompt", "resp", None),
        P("prompt", "resp", None),
        P("prompt", "resp", None, None),
        P("prompt", None),
        P(),
        P(),
        P(("prompt", "resp"), None, None),
        P(("prompt", "resp"), None, None),
        P(("prompt", "resp"), None, None),
        P("prompt", "resp", None, None),
        P("prompt", "resp"),
        P("prompt", "resp", None, None),
    )
    out_specs = (
        P("prompt", "resp", None, None),
        P("prompt", "resp", None, None),
        P("prompt", "resp", None, None),
        P("prompt", "resp", None, None),
        P("prompt", "resp", None, None),
        P("prompt", "resp", None),
        P("prompt", "resp", None),
        P(),
        P(),
        P(("prompt", "resp"), None, None),
        P(("prompt", "resp"), None, None),
        P(("prompt", "resp"), None, None),
    )
    return jax.shard_map(shards, mesh=mesh, in_specs=in_specs, out_specs=out_specs, check_vma=False)
```
